512 devices in a mesh: seq: 32 (over y, x), head: 16 (over z, core).
Axes of the slice: x: 4, y: 8, z: 8, core: 2. Of those that a mesh axis runs over, the one named last changes fastest.
Arguments:
- queries: bfloat16 [65536, 4096], P(('seq', 'head')), may hold values from -2.59375 to 2.59375
- key_matrix: bfloat16 [65536, 512], P(('seq', 'head')), may hold values from -2.59375 to 2.59375
- value_matrix: bfloat16 [65536, 512], P(('seq', 'head')), may hold values from -6 to 6
- attn_output: bfloat16 [65536, 4096], P(('seq', 'head')), may hold values from -6 to 6
- grad_output: bfloat16 [65536, 4096], P(('seq', 'head')), may hold values from -6 to 6
- prefix_len: int32 [32], replicated, may hold values from 1 to 128, as said below
- rollout_len: int32 [32, 15], replicated, may hold values from 1 to 128, as said below
- rollout_prompt: int32 [480, 1], replicated, may hold values from 0 to 31
- prefix_owner: int32 [32], replicated, may hold values from 0 to 31, each once
Outputs:
- grad_query: bfloat16 [65536, 4096], P(('seq', 'head'))
- key_gradient: bfloat16 [65536, 512], P(('seq', 'head'))
- value_gradient: bfloat16 [65536, 512], P(('seq', 'head'))
The draws below stay inside these ranges and needn't reach their ends.
Inputs may be any that keep to these rules, and one draw needn't show every extreme that they name: `prefix_len`: some prompt's prefix is live in all 128 rows. `rollout_len`: some slot is live in all 128 rows. `rollout_prompt`: every prompt has at least one rollout slot. `prefix_owner`: each shard stores exactly one prefix.
All inputs are finite; a program needn't handle non-finite values.
Results may differ from the reference program's by a relative error of at most 0.0054.
Values may be sent and summed in bfloat16 or wider, within the bound.
A program may use at most 64 MiB of HBM per device.

```python
import math
import jax
import jax.numpy as jnp
from jax import lax

QUERY_HEADS = 32
KEY_VALUE_HEADS = 4
HEAD_SIZE = 128
PREFIX_ROWS = 128
RLEN = 128
SHARD_ROWS = 2048
ROLLOUT_SLOTS = 15
PACK_ROWS = 65536
ROLLOUTS = 480
N_SEQ = 32


def draw_prefix_len(key, part):
    key = jax.random.fold_in(key, 11)
    draw_key, pick_key = jax.random.split(key)
    lengths = jax.random.randint(draw_key, (N_SEQ,), 1, PREFIX_ROWS + 1)
    chosen = jax.random.randint(pick_key, (), 0, N_SEQ)
    return jnp.where(jnp.arange(N_SEQ) == chosen, PREFIX_ROWS, lengths).astype(jnp.int32)


def draw_rollout_len(key, part):
    key = jax.random.fold_in(key, 23)
    draw_key, pick_key = jax.random.split(key)
    lengths = jax.random.randint(draw_key, (N_SEQ * ROLLOUT_SLOTS,), 1, RLEN + 1)
    chosen = jax.random.randint(pick_key, (), 0, N_SEQ * ROLLOUT_SLOTS)
    filled = jnp.where(jnp.arange(N_SEQ * ROLLOUT_SLOTS) == chosen, RLEN, lengths)
    return filled.reshape(N_SEQ, ROLLOUT_SLOTS).astype(jnp.int32)


def block_scale(stream_key, extent, cuts, least, largest):
    level, own = 1.0, jax.random.fold_in(stream_key, 6)
    for axis_at, shards_of in cuts:
        steps = jnp.exp(jax.random.uniform(jax.random.fold_in(own, axis_at), (shards_of,), jnp.float32, least / len(cuts), largest / len(cuts)))
        level = level * jnp.repeat(steps, extent[axis_at] // shards_of).reshape([-1 if axis == axis_at else 1 for axis in range(len(extent))])
    return level


def choose_distinct(own_key, rows, number_of, top, lift):
    order = jax.random.permutation(jax.random.fold_in(own_key, 1), number_of)
    favour = order
    for power in range(3):
        favour = favour * favour // number_of
    favour = favour * lift // number_of
    lots = jax.random.randint(jax.random.fold_in(own_key, 2), (rows, number_of), 0, 4096) + favour
    holders = jax.random.permutation(jax.random.fold_in(own_key, 3), rows)[jnp.arange(number_of) % rows]
    lots = jnp.where(jnp.arange(rows)[:, None] == holders[None, :], 1 << 14, lots)
    score = lots * number_of + jnp.arange(number_of)
    return lax.top_k(score.astype(jnp.int32), top)[1].astype(jnp.int32)


def bell_draw(stream_key, shape, deviation, reach, cuts=(), kind=jnp.bfloat16):
    array = jax.random.normal(stream_key, shape, jnp.float32) * deviation
    if len(cuts) > 0:
        array = block_scale(stream_key, shape, cuts, -0.22, 0.18) * array
    return jnp.clip(array, min=-reach, max=reach).astype(kind)


def setup_inputs(seed: int = 0) -> dict:
    key_of = jax.random.split(jax.random.key(seed), 10)
    return {
        "queries": bell_draw(key_of[0], (PACK_ROWS, QUERY_HEADS * HEAD_SIZE), 1.0, 2.59375, ((0, 512),)),
        "key_matrix": bell_draw(key_of[1], (PACK_ROWS, KEY_VALUE_HEADS * HEAD_SIZE), 1.0, 2.59375, ((0, 512),)),
        "value_matrix": bell_draw(key_of[2], (PACK_ROWS, KEY_VALUE_HEADS * HEAD_SIZE), 1.0, 6.0, ((0, 512),)),
        "attn_output": bell_draw(key_of[3], (PACK_ROWS, QUERY_HEADS * HEAD_SIZE), 1.0, 6.0, ((0, 512),)),
        "grad_output": bell_draw(key_of[4], (PACK_ROWS, QUERY_HEADS * HEAD_SIZE), 1.0, 6.0, ((0, 512),)),
        "prefix_len": draw_prefix_len(jax.random.fold_in(key_of[9], 71), 0),
        "rollout_len": draw_rollout_len(jax.random.fold_in(key_of[9], 71), 0),
        "rollout_prompt": choose_distinct(key_of[7], ROLLOUTS, N_SEQ, 1, 512),
        "prefix_owner": jax.random.permutation(key_of[8], N_SEQ).astype(jnp.int32),
    }


def attend(query_rows, grad_rows, delta_rows, key_rows, value_rows, allowed):
    factor = 1.0 / math.sqrt(HEAD_SIZE)
    query_wide = query_rows.astype(jnp.float32)
    grad_wide = grad_rows.astype(jnp.float32)
    key_wide = key_rows.astype(jnp.float32)
    value_wide = value_rows.astype(jnp.float32)
    scores = jnp.einsum('rhd,khd->hrk', query_wide, key_wide) * factor
    raised = jnp.where(allowed[None], jnp.exp(scores), 0.0)
    row_total = lax.optimization_barrier(jnp.sum(raised, axis=-1, keepdims=True))
    live_rows = jnp.any(allowed, axis=-1)[None, :, None]
    weights = raised / jnp.where(live_rows, row_total, 1.0)
    weights_low = lax.optimization_barrier(weights.astype(jnp.bfloat16)).astype(jnp.float32)
    value_gradient = jnp.einsum('hrk,rhd->khd', weights_low, grad_wide)
    grad_weights = jnp.einsum('rhd,khd->hrk', grad_wide, value_wide)
    grad_scores = weights * (grad_weights - jnp.transpose(delta_rows)[:, :, None])
    scores_low = lax.optimization_barrier(grad_scores.astype(jnp.bfloat16)).astype(jnp.float32)
    grad_query = jnp.einsum('hrk,khd->rhd', scores_low, key_wide) * factor
    key_gradient = jnp.einsum('hrk,rhd->khd', scores_low, query_wide) * factor
    return (grad_query, key_gradient, value_gradient)

def prefix_mask(live_count):
    positions = jnp.arange(PREFIX_ROWS, dtype=jnp.int32)
    return (positions[None, :] <= positions[:, None]) & (positions[:, None] < live_count)

def slot_mask(prefix_count, live_count):
    rows_here = jnp.arange(RLEN, dtype=jnp.int32)
    columns = jnp.arange(PREFIX_ROWS, dtype=jnp.int32)
    live_rows = rows_here < live_count
    remote = live_rows[:, None] & (columns[None, :] < prefix_count)
    local = live_rows[:, None] & (rows_here[None, :] <= rows_here[:, None])
    return jnp.concatenate([remote, local], axis=1)

def reference(queries, key_matrix, value_matrix, attn_output, grad_output, prefix_len, rollout_len, rollout_prompt, prefix_owner):
    group_width = QUERY_HEADS // KEY_VALUE_HEADS
    query_all = queries.reshape(N_SEQ, SHARD_ROWS, QUERY_HEADS, HEAD_SIZE)
    grad_all = grad_output.reshape(N_SEQ, SHARD_ROWS, QUERY_HEADS, HEAD_SIZE)
    output_all = attn_output.reshape(N_SEQ, SHARD_ROWS, QUERY_HEADS, HEAD_SIZE)
    gathered_keys = key_matrix.reshape(N_SEQ, SHARD_ROWS, KEY_VALUE_HEADS, HEAD_SIZE)
    gathered_values = value_matrix.reshape(N_SEQ, SHARD_ROWS, KEY_VALUE_HEADS, HEAD_SIZE)
    prompt_list = rollout_prompt[:, 0].astype(jnp.int32)

    def one_shard(shard):
        query_rows = query_all[shard]
        grad_rows = grad_all[shard]
        products = grad_rows.astype(jnp.float32) * output_all[shard].astype(jnp.float32)
        delta_rows = lax.optimization_barrier(lax.optimization_barrier(jnp.sum(products, axis=-1)).astype(jnp.bfloat16)).astype(jnp.float32)
        key_rows = jnp.repeat(gathered_keys[shard], group_width, axis=1)
        value_rows = jnp.repeat(gathered_values[shard], group_width, axis=1)
        own_len = jnp.sum(jnp.where(prefix_owner == shard, prefix_len, 0))
        pre_query, pre_key, pre_value = attend(query_rows[:PREFIX_ROWS], grad_rows[:PREFIX_ROWS], delta_rows[:PREFIX_ROWS], key_rows[:PREFIX_ROWS], value_rows[:PREFIX_ROWS], prefix_mask(own_len))
        prompts = lax.dynamic_slice_in_dim(prompt_list, (shard * ROLLOUT_SLOTS).astype(jnp.int32), ROLLOUT_SLOTS)
        live_lens = rollout_len[shard]

        def one_slot(slot):
            prompt = prompts[slot]
            source = prefix_owner[prompt]
            remote_key = jnp.repeat(gathered_keys[source, :PREFIX_ROWS], group_width, axis=1)
            remote_value = jnp.repeat(gathered_values[source, :PREFIX_ROWS], group_width, axis=1)
            start = (PREFIX_ROWS + slot * RLEN).astype(jnp.int32)
            slot_query = lax.dynamic_slice_in_dim(query_rows, start, RLEN, 0)
            slot_grad = lax.dynamic_slice_in_dim(grad_rows, start, RLEN, 0)
            slot_delta = lax.dynamic_slice_in_dim(delta_rows, start, RLEN, 0)
            slot_key = lax.dynamic_slice_in_dim(key_rows, start, RLEN, 0)
            slot_value = lax.dynamic_slice_in_dim(value_rows, start, RLEN, 0)
            allowed = slot_mask(prefix_len[prompt], live_lens[slot])
            out_query, out_key, out_value = attend(slot_query, slot_grad, slot_delta, jnp.concatenate([remote_key, slot_key], axis=0), jnp.concatenate([remote_value, slot_value], axis=0), allowed)
            return (out_query, out_key[PREFIX_ROWS:], out_value[PREFIX_ROWS:], out_key[:PREFIX_ROWS], out_value[:PREFIX_ROWS])
        slot_query, slot_key, slot_value, distant_key, distant_value = lax.map(one_slot, jnp.arange(ROLLOUT_SLOTS, dtype=jnp.int32))
        complete_query = jnp.concatenate([pre_query, slot_query.reshape(ROLLOUT_SLOTS * RLEN, QUERY_HEADS, HEAD_SIZE)], axis=0).astype(jnp.bfloat16)
        complete_key = jnp.concatenate([pre_key, slot_key.reshape(ROLLOUT_SLOTS * RLEN, QUERY_HEADS, HEAD_SIZE)], axis=0)
        complete_value = jnp.concatenate([pre_value, slot_value.reshape(ROLLOUT_SLOTS * RLEN, QUERY_HEADS, HEAD_SIZE)], axis=0)
        complete_key = lax.optimization_barrier(jnp.sum(complete_key.reshape(SHARD_ROWS, KEY_VALUE_HEADS, group_width, HEAD_SIZE), axis=2))
        complete_value = lax.optimization_barrier(jnp.sum(complete_value.reshape(SHARD_ROWS, KEY_VALUE_HEADS, group_width, HEAD_SIZE), axis=2))
        distant_key = lax.optimization_barrier(jnp.sum(distant_key.reshape(ROLLOUT_SLOTS, PREFIX_ROWS, KEY_VALUE_HEADS, group_width, HEAD_SIZE), axis=3))
        distant_value = lax.optimization_barrier(jnp.sum(distant_value.reshape(ROLLOUT_SLOTS, PREFIX_ROWS, KEY_VALUE_HEADS, group_width, HEAD_SIZE), axis=3))
        return (complete_query, complete_key, complete_value, distant_key, distant_value)
    complete_query, complete_key, complete_value, distant_key, distant_value = lax.map(one_shard, jnp.arange(N_SEQ, dtype=jnp.int32))
    destinations = prefix_owner[prompt_list]
    owning_shards = (destinations[:, None] == jnp.arange(N_SEQ, dtype=jnp.int32)[None, :]).astype(jnp.float32)
    key_addend = jnp.einsum('iq,iz->qz', owning_shards, distant_key.reshape(N_SEQ * ROLLOUT_SLOTS, -1), precision=lax.Precision.HIGHEST).reshape(N_SEQ, PREFIX_ROWS, KEY_VALUE_HEADS, HEAD_SIZE)
    value_addend = jnp.einsum('iq,iz->qz', owning_shards, distant_value.reshape(N_SEQ * ROLLOUT_SLOTS, -1), precision=lax.Precision.HIGHEST).reshape(N_SEQ, PREFIX_ROWS, KEY_VALUE_HEADS, HEAD_SIZE)
    key_gradient = complete_key.at[:, :PREFIX_ROWS].add(key_addend)
    value_gradient = complete_value.at[:, :PREFIX_ROWS].add(value_addend)
    return (complete_query.reshape(PACK_ROWS, QUERY_HEADS * HEAD_SIZE), key_gradient.astype(jnp.bfloat16).reshape(PACK_ROWS, KEY_VALUE_HEADS * HEAD_SIZE), value_gradient.astype(jnp.bfloat16).reshape(PACK_ROWS, KEY_VALUE_HEADS * HEAD_SIZE))
```

```python
import functools
import math

import jax
import jax.numpy as jnp
from jax import lax
from jax.experimental import pallas as pl
from jax.experimental.pallas import tpu as pltpu
from jax.sharding import PartitionSpec as P

QUERY_HEADS = 32
KEY_VALUE_HEADS = 4
HEAD_SIZE = 128
PREFIX_ROWS = 128
RLEN = 128
MESH = pl.DeviceIdType.MESH
F32 = jnp.float32
BF16 = jnp.bfloat16
VMEM_BYTES = 60 * 1024 * 1024


def mm(a, b, da, db):
    return lax.dot_general(a, b, (((da,), (db,)), ((), ())), preferred_element_type=F32)


def kernel(
    ny,
    nx,
    nt,
    prompt_ref,
    owner_ref,
    plen_ref,
    rlen_ref,
    q_hbm,
    k_hbm,
    v_hbm,
    o_hbm,
    do_hbm,
    dq_hbm,
    dk_hbm,
    dv_hbm,
    q,
    k,
    v,
    o,
    do,
    dq,
    dk,
    dv,
    strip,
    units,
    picked,
    pre,
    back_out,
    back,
    sums,
    parts,
    final,
    spread,
    exps,
    prods,
    ds_pre,
    w_low,
    ds_low,
    delta,
    total,
    in_sem,
    out_sem,
    send_sem,
    recv_sem,
):
    n_seq = ny * nx
    group = nx * nt
    heads = q.shape[1] // (nx * HEAD_SIZE)
    unit_rows = PREFIX_ROWS // (nt // 2)
    width = heads * HEAD_SIZE
    factor = 1.0 / math.sqrt(HEAD_SIZE)
    s = lax.axis_index("seq")
    t = lax.axis_index("head")
    y = s // nx
    x = s % nx
    kind = t % 2
    block = t // 2

    def each(count, body, start=0):
        def step(i, carry):
            body(i)
            return carry

        lax.fori_loop(start, count, step, 0)

    loads = [
        pltpu.make_async_copy(a, b, in_sem.at[i])
        for i, (a, b) in enumerate(((q_hbm, q), (k_hbm, k), (v_hbm, v), (do_hbm, do), (o_hbm, o)))
    ]
    for load in loads:
        load.start()

    barrier = pltpu.get_barrier_semaphore()

    def greet_row(i):
        peer = (y * nx + (x + i // nt) % nx, (t + i) % nt)
        pl.semaphore_signal(barrier, inc=1, device_id=peer, device_id_type=MESH)

    def greet_plane(i):
        peer = (((y + 1 + i // nx) % ny) * nx + i % nx, t)
        pl.semaphore_signal(barrier, inc=1, device_id=peer, device_id_type=MESH)

    each(group, greet_row, 1)
    each((ny - 1) * nx, greet_plane)
    pl.semaphore_wait(barrier, group - 1 + (ny - 1) * nx)

    def remote(src, dst, stage, peer):
        return pltpu.make_async_remote_copy(
            src_ref=src,
            dst_ref=dst,
            send_sem=send_sem.at[stage],
            recv_sem=recv_sem.at[stage],
            device_id=peer,
            device_id_type=MESH,
        )

    def local(src, dst, stage):
        return pltpu.make_async_copy(src, dst, recv_sem.at[stage])

    def arrived(ref, stage):
        pltpu.make_async_copy(ref, ref, recv_sem.at[stage]).wait()

    def sent(ref, stage):
        pltpu.make_async_copy(ref, ref, send_sem.at[stage]).wait()

    @pl.when(t == 0)
    def _():
        local(k_hbm.at[pl.ds(0, unit_rows)], strip, 0).start()
        remote(v_hbm.at[pl.ds(0, unit_rows)], strip, 0, (s, 1)).start()

        def send_strips(i):
            rows = pl.ds(pl.multiple_of(i * unit_rows, unit_rows), unit_rows)
            remote(k_hbm.at[rows], strip, 0, (s, 2 * i)).start()
            remote(v_hbm.at[rows], strip, 0, (s, 2 * i + 1)).start()

        each(nt // 2, send_strips, 1)

    def source(x2, t2):
        at = (y * nx + x2) * (nt - 1) + jnp.maximum(t2 - 1, 0)
        return jnp.where(t2 == 0, y * nx + x2, owner_ref[prompt_ref[at]])

    lane = lax.broadcasted_iota(jnp.int32, (8, group * unit_rows), 1)

    def note_source(i, line):
        return jnp.where(lane // unit_rows == i, source(i // nt, i % nt), line)

    source_line = lax.fori_loop(0, group, note_source, jnp.zeros_like(lane))
    shape = (unit_rows, group * unit_rows)
    same_row = (
        lax.broadcasted_iota(jnp.int32, shape, 0)
        == lax.broadcasted_iota(jnp.int32, shape, 1) % unit_rows
    )
    keyed = jnp.where(same_row, jnp.broadcast_to(source_line[:1], shape), -1)

    def spread_rows(i):
        spread[pl.ds(pl.multiple_of(i * unit_rows, unit_rows), unit_rows), :] = jnp.where(
            keyed == i, 1.0, 0.0
        ).astype(BF16)

    each(n_seq, spread_rows)

    is_prefix = t == 0
    mine = s * (nt - 1) + jnp.maximum(t - 1, 0)
    own_len = lax.fori_loop(
        0, n_seq, lambda i, n: n + jnp.where(owner_ref[i] == s, plen_ref[i], 0), jnp.int32(0)
    )
    live = jnp.where(is_prefix, own_len, rlen_ref[jnp.maximum(t - 1, 0), s])
    live_local = jnp.where(is_prefix, 0, live)
    prefix_count = jnp.where(is_prefix, PREFIX_ROWS, plen_ref[prompt_ref[mine]])
    slack = jnp.where(is_prefix, 0, PREFIX_ROWS)
    pair = 2 * HEAD_SIZE
    key_at = lax.broadcasted_iota(jnp.int32, (RLEN, pair), 0)
    row_at = lax.broadcasted_iota(jnp.int32, (RLEN, pair), 1) % RLEN
    row_line = lax.broadcasted_iota(jnp.int32, (1, pair), 1) % RLEN

    def columns(ref, g, p):
        at = pl.multiple_of(g * width + p * pair, HEAD_SIZE)
        return jnp.concatenate(
            [ref[:, pl.ds(at, HEAD_SIZE)], ref[:, pl.ds(at + HEAD_SIZE, HEAD_SIZE)]], axis=0
        )

    def head_columns(ref, g):
        return ref[:, pl.ds(pl.multiple_of(g * HEAD_SIZE, HEAD_SIZE), HEAD_SIZE)]

    def powers(key_rows, query_rows, allowed):
        scores = mm(key_rows, query_rows, 1, 1) * (factor * math.log2(math.e))
        return jnp.where(allowed, jnp.exp2(scores), 0.0)

    def own_part(g):
        allowed = (key_at <= row_at) & (row_at < live_local)
        key_rows, value_rows = head_columns(k, g), head_columns(v, g)
        ones = jnp.ones((8, HEAD_SIZE), BF16)
        for p in range(heads // 2):
            at = pl.ds(p * pair, pair)
            grad_rows = columns(do, g, p)
            product = grad_rows.astype(F32) * columns(o, g, p).astype(F32)
            high = product.astype(BF16)
            low = (product - high.astype(F32)).astype(BF16)
            deltas = (mm(ones, high, 1, 1) + mm(ones, low, 1, 1)).astype(BF16).astype(F32)
            delta[g, :, at] = deltas
            raised = powers(key_rows, columns(q, g, p), allowed)
            total[g, :, at] = jnp.broadcast_to(jnp.sum(raised, axis=0, keepdims=True), (8, pair))
            exps[g, :, at] = raised
            prods[g, :, at] = raised * (mm(value_rows, grad_rows, 1, 1) - deltas[:1])

    def stack(ref, g):
        at = pl.multiple_of(g * width, HEAD_SIZE)
        return jnp.concatenate(
            [ref[:, pl.ds(at + h * HEAD_SIZE, HEAD_SIZE)] for h in range(heads)], axis=0
        )

    arrived(strip, 0)

    def unit_of(x2):
        return strip.at[:, pl.ds(pl.multiple_of(x2 * HEAD_SIZE, HEAD_SIZE), HEAD_SIZE)]

    local(unit_of(x), units.at[s], 1).start()

    def send_unit(i):
        x2, y2 = (x + i) % nx, (y + i // nx) % ny
        remote(unit_of(x2), units.at[s], 1, (y2 * nx + x2, t)).start()

    each(n_seq, send_unit, 1)

    for load in loads:
        load.wait()
    own_part(0)
    each(nx // 2, own_part, 1)

    arrived(units, 1)

    def pick(i):
        picked[i] = units[source(i // nt, i % nt)]

    each(group, pick)

    def landing(ref):
        return ref.at[kind, x, pl.ds(pl.multiple_of(block * unit_rows, unit_rows), unit_rows)]

    local(picked.at[x * nt + t], landing(pre), 2).start()

    def send_picked(i):
        x2, t2 = (x + i // nt) % nx, (t + i) % nt
        remote(picked.at[x2 * nt + t2], landing(pre), 2, (y * nx + x2, t2)).start()

    each(group, send_picked, 1)
    each(nx, own_part, nx // 2)
    arrived(pre, 2)

    def prefix_part(j):
        g = (x + j) % nx
        allowed = (row_at < live) & (key_at < prefix_count) & (key_at <= row_at + slack)
        key_rows, value_rows = pre[0, g], pre[1, g]
        for p in range(heads // 2):
            at = pl.ds(p * pair, pair)
            raised = powers(key_rows, columns(q, g, p), allowed)
            row_total = total[g, :1, at] + jnp.sum(raised, axis=0, keepdims=True)
            inverse = 1.0 / jnp.where(row_line < live, row_total, 1.0)
            total[g, :, at] = jnp.broadcast_to(inverse, (8, pair))
            weights = raised * inverse
            w_low[:, at] = weights.astype(BF16)
            grad_weights = mm(value_rows, columns(do, g, p), 1, 1)
            ds_pre[g, :, at] = (weights * (grad_weights - delta[g, :1, at])).astype(BF16)
        back_out[1, g] = mm(w_low[...], stack(do, g), 1, 0).astype(BF16)
        back_out[0, g] = (mm(ds_pre[g], stack(q, g), 1, 0) * factor).astype(BF16)

        def send_back(i):
            t2 = (t + i) % nt
            unit = back_out.at[
                t2 % 2, g, pl.ds(pl.multiple_of((t2 // 2) * unit_rows, unit_rows), unit_rows)
            ]
            here = (j == 0) & (i == 0)

            @pl.when(here)
            def _():
                local(unit, back.at[x * nt + t], 3).start()

            @pl.when(jnp.logical_not(here))
            def _():
                remote(unit, back.at[x * nt + t], 3, (y * nx + g, t2)).start()

        each(nt, send_back)

    each(nx, prefix_part)

    def rest(g):
        key_rows, prefix_rows = head_columns(k, g), pre[0, g]
        for p in range(heads // 2):
            at = pl.ds(p * pair, pair)
            inverse = total[g, :1, at]
            w_low[:, at] = (exps[g, :, at] * inverse).astype(BF16)
            low = (prods[g, :, at] * inverse).astype(BF16)
            ds_low[:, at] = low
            grads = mm(ds_pre[g, :, at], prefix_rows, 0, 0) + mm(low, key_rows, 0, 0)
            grads = (grads * factor).astype(BF16)
            to = pl.multiple_of(g * width + p * pair, HEAD_SIZE)
            dq[:, pl.ds(to, HEAD_SIZE)] = grads[:RLEN]
            dq[:, pl.ds(to + HEAD_SIZE, HEAD_SIZE)] = grads[RLEN:]
        to = pl.ds(pl.multiple_of(g * HEAD_SIZE, HEAD_SIZE), HEAD_SIZE)
        dv[:, to] = mm(w_low[...], stack(do, g), 1, 0).astype(BF16)
        dk[:, to] = (mm(ds_low[...], stack(q, g), 1, 0) * factor).astype(BF16)

    each(nx, rest)
    store_query = pltpu.make_async_copy(dq, dq_hbm, out_sem.at[0])
    store_query.start()

    @pl.when(t != 0)
    def _():
        pltpu.make_async_copy(dk, dk_hbm, out_sem.at[1]).start()
        pltpu.make_async_copy(dv, dv_hbm, out_sem.at[2]).start()

    arrived(back, 3)
    gathered = back[...].reshape(group * unit_rows, HEAD_SIZE)
    sums[...] = mm(spread[...], gathered, 1, 0).astype(BF16).reshape(sums.shape)
    local(sums.at[s], parts.at[s], 4).start()

    def send_sum(i):
        x2, y2 = (x + i) % nx, (y + i // nx) % ny
        remote(sums.at[y2 * nx + x2], parts.at[s], 4, (y2 * nx + x2, t)).start()

    each(n_seq, send_sum, 1)
    arrived(parts, 4)
    for h in range(nx):
        whole = parts[h].astype(F32)
        for i in range(1, ny):
            whole += parts[i * nx + h].astype(F32)
        final[:, pl.ds(h * HEAD_SIZE, HEAD_SIZE)] = whole.astype(BF16)

    rows = pl.ds(pl.multiple_of(block * unit_rows, unit_rows), unit_rows)

    @pl.when(t == 0)
    def _():
        local(final, dk_hbm.at[rows], 5).start()

    @pl.when((t != 0) & (kind == 0))
    def _():
        remote(final, dk_hbm.at[rows], 5, (s, 0)).start()

    @pl.when(kind == 1)
    def _():
        remote(final, dv_hbm.at[rows], 6, (s, 0)).start()

    store_query.wait()
    sent(units.at[pl.ds(0, n_seq - 1)], 1)
    sent(picked.at[pl.ds(0, group - 1)], 2)
    sent(back.at[pl.ds(0, group - 1)], 3)
    sent(sums.at[pl.ds(0, n_seq - 1)], 4)

    @pl.when(t == 0)
    def _():
        sent(picked.at[pl.ds(0, (nt - 1) * nx)], 0)
        arrived(dk, 5)
        arrived(dv, 6)

    @pl.when((t != 0) & (kind == 0))
    def _():
        sent(final, 5)

    @pl.when(kind == 1)
    def _():
        sent(final, 6)

    @pl.when(t != 0)
    def _():
        pltpu.make_async_copy(dk, dk_hbm, out_sem.at[1]).wait()
        pltpu.make_async_copy(dv, dv_hbm, out_sem.at[2]).wait()


def shards(
    queries,
    key_matrix,
    value_matrix,
    attn_output,
    grad_output,
    prefix_len,
    rollout_len,
    rollout_prompt,
    prefix_owner,
):
    nt = lax.axis_size("head")
    n_seq = lax.axis_size("seq")
    nx = KEY_VALUE_HEADS
    ny = n_seq // nx
    group = nx * nt
    heads = QUERY_HEADS // nx
    width = heads * HEAD_SIZE
    unit_rows = PREFIX_ROWS // (nt // 2)
    unit = (unit_rows, HEAD_SIZE)
    anywhere = pl.BlockSpec(memory_space=pl.ANY)
    scalars = pl.BlockSpec(memory_space=pltpu.SMEM)
    wide = pltpu.VMEM(queries.shape, BF16)
    narrow = pltpu.VMEM(key_matrix.shape, BF16)
    per_head = (nx, RLEN, width)
    return pl.pallas_call(
        functools.partial(kernel, ny, nx, nt),
        out_shape=[
            jax.ShapeDtypeStruct(queries.shape, BF16),
            jax.ShapeDtypeStruct(key_matrix.shape, BF16),
            jax.ShapeDtypeStruct(value_matrix.shape, BF16),
        ],
        in_specs=[scalars] * 4 + [anywhere] * 5,
        out_specs=[anywhere] * 3,
        scratch_shapes=[
            wide,
            narrow,
            narrow,
            wide,
            wide,
            wide,
            narrow,
            narrow,
            pltpu.VMEM((unit_rows, nx * HEAD_SIZE), BF16),
            pltpu.VMEM((n_seq,) + unit, BF16),
            pltpu.VMEM((group,) + unit, BF16),
            pltpu.VMEM((2, nx, PREFIX_ROWS, HEAD_SIZE), BF16),
            pltpu.VMEM((2, nx, PREFIX_ROWS, HEAD_SIZE), BF16),
            pltpu.VMEM((group,) + unit, BF16),
            pltpu.VMEM((n_seq,) + unit, BF16),
            pltpu.VMEM((n_seq,) + unit, BF16),
            pltpu.VMEM((unit_rows, nx * HEAD_SIZE), BF16),
            pltpu.VMEM((n_seq * unit_rows, group * unit_rows), BF16),
            pltpu.VMEM(per_head, F32),
            pltpu.VMEM(per_head, F32),
            pltpu.VMEM(per_head, BF16),
            pltpu.VMEM(per_head[1:], BF16),
            pltpu.VMEM(per_head[1:], BF16),
            pltpu.VMEM((nx, 8, width), F32),
            pltpu.VMEM((nx, 8, width), F32),
            pltpu.SemaphoreType.DMA((5,)),
            pltpu.SemaphoreType.DMA((3,)),
            pltpu.SemaphoreType.DMA((7,)),
            pltpu.SemaphoreType.DMA((7,)),
        ],
        compiler_params=pltpu.CompilerParams(
            collective_id=0, has_side_effects=True, vmem_limit_bytes=VMEM_BYTES
        ),
        name="attention_backward",
    )(
        rollout_prompt.reshape(-1),
        prefix_owner,
        prefix_len,
        rollout_len.T,
        queries,
        key_matrix,
        value_matrix,
        attn_output,
        grad_output,
    )


def solution(mesh):
    rows = P(("seq", "head"), None)
    return jax.shard_map(
        shards,
        mesh=mesh,
        in_specs=(rows,) * 5 + (P(),) * 4,
        out_specs=(rows,) * 3,
        check_vma=False,
    )
```

```python
import functools
import math

import jax
import jax.numpy as jnp
from jax import lax
from jax.experimental import pallas as pl
from jax.experimental.pallas import tpu as pltpu
from jax.sharding import PartitionSpec as P

QUERY_HEADS = 32
KEY_VALUE_HEADS = 4
HEAD_SIZE = 128
PREFIX_ROWS = 128
RLEN = 128
MESH = pl.DeviceIdType.MESH
F32 = jnp.float32
BF16 = jnp.bfloat16
VMEM_BYTES = 56 * 1024 * 1024


def mm(a, b, da, db):
    return lax.dot_general(a, b, (((da,), (db,)), ((), ())), preferred_element_type=F32)


def kernel(
    ny,
    nx,
    nt,
    prompt_ref,
    owner_ref,
    plen_ref,
    rlen_ref,
    q_hbm,
    k_hbm,
    v_hbm,
    o_hbm,
    do_hbm,
    dq,
    dk,
    dv,
    q,
    k,
    v,
    o,
    do,
    strip,
    cut,
    units,
    picked,
    pre,
    back_out,
    back,
    sums,
    parts,
    final,
    spread,
    partial,
    sources,
    exps,
    prods,
    ds_pre,
    w_low,
    ds_low,
    delta,
    total,
    in_sem,
    send_sem,
    recv_sem,
):
    n_seq = ny * nx
    group = nx * nt
    heads = q.shape[1] // (nx * HEAD_SIZE)
    unit_rows = PREFIX_ROWS // (nt // 2)
    width = heads * HEAD_SIZE
    factor = 1.0 / math.sqrt(HEAD_SIZE)
    s = lax.axis_index("seq")
    t = lax.axis_index("head")
    y, x = lax.div(s, nx), lax.rem(s, nx)
    block, kind = lax.div(t, 2), lax.rem(t, 2)

    def each(count, body, start=0):
        def step(i, carry):
            body(i)
            return carry

        lax.fori_loop(start, count, step, 0)

    loads = [
        pltpu.make_async_copy(a, b, in_sem.at[i])
        for i, (a, b) in enumerate(((q_hbm, q), (k_hbm, k), (v_hbm, v), (do_hbm, do), (o_hbm, o)))
    ]
    for load in loads:
        load.start()

    barrier = pltpu.get_barrier_semaphore()

    nz = nt // 2
    xs = [lax.rem(x + i, nx) for i in range(nx)]
    ys = [lax.rem(y + i, ny) for i in range(ny)]
    zs = [lax.rem(block + i, nz) for i in range(nz)]
    cs = [kind, 1 - kind]

    def far_first(n):
        return sorted(range(n), key=lambda i: (-min(i, n - i), i))

    plane = [(i, j) for i in range(ny) for j in range(nx) if i + j > 0]
    plane.sort(key=lambda at: -min(at[0], ny - at[0]) - min(at[1], nx - at[1]))
    column = [(j, c) for j in far_first(nz) for c in (1, 0)]

    def greet(peer):
        pl.semaphore_signal(barrier, inc=1, device_id=peer, device_id_type=MESH)

    for i in far_first(nx):
        for j, c in column:
            if i + j + c > 0:
                greet((y * nx + xs[i], zs[j] * 2 + cs[c]))
    for i, j in plane:
        if i > 0:
            greet((ys[i] * nx + xs[j], t))
    pl.semaphore_wait(barrier, group - 1 + (ny - 1) * nx)

    def remote(src, dst, stage, peer):
        return pltpu.make_async_remote_copy(
            src_ref=src,
            dst_ref=dst,
            send_sem=send_sem.at[stage],
            recv_sem=recv_sem.at[stage],
            device_id=peer,
            device_id_type=MESH,
        )

    def local(src, dst, stage):
        return pltpu.make_async_copy(src, dst, recv_sem.at[stage])

    def arrived(ref, stage):
        pltpu.make_async_copy(ref, ref, recv_sem.at[stage]).wait()

    def sent(ref, stage):
        pltpu.make_async_copy(ref, ref, send_sem.at[stage]).wait()

    @pl.when(t == 0)
    def _():
        for i in far_first(nz):
            rows = pl.ds(i * unit_rows, unit_rows)
            if i > 0:
                remote(k_hbm.at[rows], strip, 0, (s, 2 * i)).start()
            else:
                local(k_hbm.at[rows], strip, 0).start()
            remote(v_hbm.at[rows], strip, 0, (s, 2 * i + 1)).start()

    for i in range(nx):
        s2 = y * nx + xs[i]
        sources[i * nt] = s2
        for t2 in range(1, nt):
            sources[i * nt + t2] = owner_ref[prompt_ref[s2 * (nt - 1) + (t2 - 1)]]

    lane = lax.broadcasted_iota(jnp.int32, (8, group * unit_rows), 1) // unit_rows
    source_line = jnp.zeros_like(lane)
    for i in range(group):
        source_line = jnp.where(lane == i, sources[i], source_line)
    shape = (unit_rows, group * unit_rows)
    same_row = (
        lax.broadcasted_iota(jnp.int32, shape, 0)
        == lax.broadcasted_iota(jnp.int32, shape, 1) % unit_rows
    )
    keyed = jnp.where(same_row, jnp.broadcast_to(source_line[:1], shape), -1)

    def spread_rows(i):
        spread[pl.ds(pl.multiple_of(i * unit_rows, unit_rows), unit_rows), :] = jnp.where(
            keyed == i, 1.0, 0.0
        ).astype(BF16)

    each(n_seq, spread_rows)

    is_prefix = t == 0
    mine = s * (nt - 1) + jnp.maximum(t - 1, 0)
    own_len = lax.fori_loop(
        0, n_seq, lambda i, n: n + jnp.where(owner_ref[i] == s, plen_ref[i], 0), jnp.int32(0)
    )
    live = jnp.where(is_prefix, own_len, rlen_ref[jnp.maximum(t - 1, 0), s])
    live_local = jnp.where(is_prefix, 0, live)
    prefix_count = jnp.where(is_prefix, PREFIX_ROWS, plen_ref[prompt_ref[mine]])
    slack = jnp.where(is_prefix, 0, PREFIX_ROWS)
    pair = 2 * HEAD_SIZE
    key_at = lax.broadcasted_iota(jnp.int32, (RLEN, pair), 0)
    row_at = lax.broadcasted_iota(jnp.int32, (RLEN, pair), 1) % RLEN
    row_line = lax.broadcasted_iota(jnp.int32, (1, pair), 1) % RLEN

    def columns(ref, g, p):
        at = pl.multiple_of(g * width + p * pair, HEAD_SIZE)
        return jnp.concatenate(
            [ref[:, pl.ds(at, HEAD_SIZE)], ref[:, pl.ds(at + HEAD_SIZE, HEAD_SIZE)]], axis=0
        )

    def head_columns(ref, g):
        return ref[:, pl.ds(pl.multiple_of(g * HEAD_SIZE, HEAD_SIZE), HEAD_SIZE)]

    def powers(key_rows, query_rows, allowed):
        scores = mm(key_rows, query_rows, 1, 1) * (factor * math.log2(math.e))
        return jnp.where(allowed, jnp.exp2(scores), 0.0)

    def own_part(g):
        allowed = (key_at <= row_at) & (row_at < live_local)
        key_rows, value_rows = head_columns(k, g), head_columns(v, g)
        ones = jnp.ones((8, HEAD_SIZE), BF16)
        for p in range(heads // 2):
            at = pl.ds(p * pair, pair)
            grad_rows = columns(do, g, p)
            product = grad_rows.astype(F32) * columns(o, g, p).astype(F32)
            high = product.astype(BF16)
            low = (product - high.astype(F32)).astype(BF16)
            deltas = (mm(ones, high, 1, 1) + mm(ones, low, 1, 1)).astype(BF16).astype(F32)
            delta[g, :, at] = deltas
            raised = powers(key_rows, columns(q, g, p), allowed)
            total[g, :, at] = jnp.broadcast_to(jnp.sum(raised, axis=0, keepdims=True), (8, pair))
            exps[g, :, at] = raised
            prods[g, :, at] = raised * (mm(value_rows, grad_rows, 1, 1) - deltas[:1])

    def stack(ref, g):
        at = pl.multiple_of(g * width, HEAD_SIZE)
        return jnp.concatenate(
            [ref[:, pl.ds(at + h * HEAD_SIZE, HEAD_SIZE)] for h in range(heads)], axis=0
        )

    arrived(strip, 0)

    for h in range(nx):
        cut[h] = strip[:, h * HEAD_SIZE : (h + 1) * HEAD_SIZE]
    local(cut.at[x], units.at[s], 1).start()
    for i, j in plane:
        remote(cut.at[xs[j]], units.at[s], 1, (ys[i] * nx + xs[j], t)).start()

    for load in loads:
        load.wait()
    own_part(0)
    each(nx // 2, own_part, 1)

    arrived(units, 1)

    landing = pre.at[kind, x, pl.ds(pl.multiple_of(block * unit_rows, unit_rows), unit_rows)]
    for i in far_first(nx):
        for t2 in range(nt):
            picked[i * nt + t2] = units[sources[i * nt + t2]]
        for j, c in column:
            t2 = zs[j] * 2 + cs[c]
            if i + j + c == 0:
                local(picked.at[t], landing, 7).start()
            else:
                remote(picked.at[i * nt + t2], landing, 7 + i, (y * nx + xs[i], t2)).start()
    each(nx, own_part, nx // 2)

    def prefix_part(i):
        g = xs[(nx - i) % nx]
        arrived(pre.at[:, g], 7 + i)
        allowed = (row_at < live) & (key_at < prefix_count) & (key_at <= row_at + slack)
        key_rows, value_rows = pre[0, g], pre[1, g]
        for p in range(heads // 2):
            at = pl.ds(p * pair, pair)
            raised = powers(key_rows, columns(q, g, p), allowed)
            row_total = total[g, :1, at] + jnp.sum(raised, axis=0, keepdims=True)
            inverse = 1.0 / jnp.where(row_line < live, row_total, 1.0)
            total[g, :, at] = jnp.broadcast_to(inverse, (8, pair))
            weights = raised * inverse
            w_low[:, at] = weights.astype(BF16)
            grad_weights = mm(value_rows, columns(do, g, p), 1, 1)
            ds_pre[g, :, at] = (weights * (grad_weights - delta[g, :1, at])).astype(BF16)
        back_out[1, g] = mm(w_low[...], stack(do, g), 1, 0).astype(BF16)
        back_out[0, g] = (mm(ds_pre[g], stack(q, g), 1, 0) * factor).astype(BF16)

        for j, c in column:
            t2 = zs[j] * 2 + cs[c]
            unit = back_out.at[
                cs[c], g, pl.ds(pl.multiple_of(zs[j] * unit_rows, unit_rows), unit_rows)
            ]
            if i + j + c == 0:
                local(unit, back.at[t], 7 + nx).start()
            else:
                remote(unit, back.at[i * nt + t], 7 + nx + i, (y * nx + g, t2)).start()

    for i in far_first(nx):
        prefix_part(i)

    def rest(g):
        key_rows, prefix_rows = head_columns(k, g), pre[0, g]
        for p in range(heads // 2):
            at = pl.ds(p * pair, pair)
            inverse = total[g, :1, at]
            w_low[:, at] = (exps[g, :, at] * inverse).astype(BF16)
            low = (prods[g, :, at] * inverse).astype(BF16)
            ds_low[:, at] = low
            grads = mm(ds_pre[g, :, at], prefix_rows, 0, 0) + mm(low, key_rows, 0, 0)
            grads = (grads * factor).astype(BF16)
            to = pl.multiple_of(g * width + p * pair, HEAD_SIZE)
            dq[:, pl.ds(to, HEAD_SIZE)] = grads[:RLEN]
            dq[:, pl.ds(to + HEAD_SIZE, HEAD_SIZE)] = grads[RLEN:]
        to = pl.ds(pl.multiple_of(g * HEAD_SIZE, HEAD_SIZE), HEAD_SIZE)

        @pl.when(t != 0)
        def _():
            dv[:, to] = mm(w_low[...], stack(do, g), 1, 0).astype(BF16)
            dk[:, to] = (mm(ds_low[...], stack(q, g), 1, 0) * factor).astype(BF16)

    each(nx, rest)

    depth = nt * unit_rows
    for n, i in enumerate(far_first(nx)):
        arrived(back.at[pl.ds(i * nt, nt)], 7 + nx + i)
        gathered = back[pl.ds(i * nt, nt)].reshape(depth, HEAD_SIZE)
        added = mm(spread[:, pl.ds(i * depth, depth)], gathered, 1, 0)
        if n > 0:
            added += partial[...]
        if n < nx - 1:
            partial[...] = added
        else:
            sums[...] = added.astype(BF16).reshape(sums.shape)
    local(sums.at[s], parts.at[s], 4).start()

    for i, j in plane:
        s2 = ys[i] * nx + xs[j]
        remote(sums.at[s2], parts.at[s], 4, (s2, t)).start()
    arrived(parts, 4)
    for h in range(nx):
        whole = parts[h].astype(F32)
        for i in range(1, ny):
            whole += parts[i * nx + h].astype(F32)
        final[:, pl.ds(h * HEAD_SIZE, HEAD_SIZE)] = whole.astype(BF16)

    rows = pl.ds(pl.multiple_of(block * unit_rows, unit_rows), unit_rows)

    @pl.when(t == 0)
    def _():
        local(final, dk.at[rows], 5).start()

    @pl.when((t != 0) & (kind == 0))
    def _():
        remote(final, dk.at[rows], 5, (s, 0)).start()

    @pl.when(kind == 1)
    def _():
        remote(final, dv.at[rows], 6, (s, 0)).start()

    sent(units.at[pl.ds(0, n_seq - 1)], 1)
    for i in range(nx):
        count = nt if i > 0 else nt - 1
        sent(picked.at[pl.ds(0, count)], 7 + i)
        sent(back.at[pl.ds(0, count)], 7 + nx + i)
    sent(sums.at[pl.ds(0, n_seq - 1)], 4)

    @pl.when(t == 0)
    def _():
        sent(picked.at[pl.ds(0, (nt - 1) * nx)], 0)
        arrived(dk, 5)
        arrived(dv, 6)

    @pl.when((t != 0) & (kind == 0))
    def _():
        sent(final, 5)

    @pl.when(kind == 1)
    def _():
        sent(final, 6)


def shards(
    queries,
    key_matrix,
    value_matrix,
    attn_output,
    grad_output,
    prefix_len,
    rollout_len,
    rollout_prompt,
    prefix_owner,
):
    nt = lax.axis_size("head")
    n_seq = lax.axis_size("seq")
    nx = KEY_VALUE_HEADS
    ny = n_seq // nx
    group = nx * nt
    heads = QUERY_HEADS // nx
    width = heads * HEAD_SIZE
    unit_rows = PREFIX_ROWS // (nt // 2)
    unit = (unit_rows, HEAD_SIZE)
    anywhere = pl.BlockSpec(memory_space=pl.ANY)
    scalars = pl.BlockSpec(memory_space=pltpu.SMEM)
    resident = pl.BlockSpec(memory_space=pltpu.VMEM)
    wide = pltpu.VMEM(queries.shape, BF16)
    narrow = pltpu.VMEM(key_matrix.shape, BF16)
    per_head = (nx, RLEN, width)
    return pl.pallas_call(
        functools.partial(kernel, ny, nx, nt),
        out_shape=[wide, narrow, narrow],
        in_specs=[scalars] * 4 + [anywhere] * 5,
        out_specs=[resident] * 3,
        scratch_shapes=[
            wide,
            narrow,
            narrow,
            wide,
            wide,
            pltpu.VMEM((unit_rows, nx * HEAD_SIZE), BF16),
            pltpu.VMEM((nx,) + unit, BF16),
            pltpu.VMEM((n_seq,) + unit, BF16),
            pltpu.VMEM((group,) + unit, BF16),
            pltpu.VMEM((2, nx, PREFIX_ROWS, HEAD_SIZE), BF16),
            pltpu.VMEM((2, nx, PREFIX_ROWS, HEAD_SIZE), BF16),
            pltpu.VMEM((group,) + unit, BF16),
            pltpu.VMEM((n_seq,) + unit, BF16),
            pltpu.VMEM((n_seq,) + unit, BF16),
            pltpu.VMEM((unit_rows, nx * HEAD_SIZE), BF16),
            pltpu.VMEM((n_seq * unit_rows, group * unit_rows), BF16),
            pltpu.VMEM((n_seq * unit_rows, HEAD_SIZE), F32),
            pltpu.SMEM((group,), jnp.int32),
            pltpu.VMEM(per_head, F32),
            pltpu.VMEM(per_head, F32),
            pltpu.VMEM(per_head, BF16),
            pltpu.VMEM(per_head[1:], BF16),
            pltpu.VMEM(per_head[1:], BF16),
            pltpu.VMEM((nx, 8, width), F32),
            pltpu.VMEM((nx, 8, width), F32),
            pltpu.SemaphoreType.DMA((5,)),
            pltpu.SemaphoreType.DMA((7 + 2 * nx,)),
            pltpu.SemaphoreType.DMA((7 + 2 * nx,)),
        ],
        compiler_params=pltpu.CompilerParams(
            collective_id=0, has_side_effects=True, vmem_limit_bytes=VMEM_BYTES
        ),
        name="attention_backward",
    )(
        rollout_prompt.reshape(-1),
        prefix_owner,
        prefix_len,
        rollout_len.T,
        queries,
        key_matrix,
        value_matrix,
        attn_output,
        grad_output,
    )


def solution(mesh):
    rows = P(("seq", "head"), None)
    return jax.shard_map(
        shards,
        mesh=mesh,
        in_specs=(rows,) * 5 + (P(),) * 4,
        out_specs=(rows,) * 3,
        check_vma=False,
    )
```

```python
import functools
import math

import jax
import jax.numpy as jnp
from jax import lax
from jax.experimental import pallas as pl
from jax.experimental.pallas import tpu as pltpu
from jax.sharding import PartitionSpec as P

QUERY_HEADS = 32
KEY_VALUE_HEADS = 4
HEAD_SIZE = 128
PREFIX_ROWS = 128
RLEN = 128
MESH = pl.DeviceIdType.MESH
F32 = jnp.float32
BF16 = jnp.bfloat16
VMEM_BYTES = 56 * 1024 * 1024


def mm(a, b, da, db):
    return lax.dot_general(a, b, (((da,), (db,)), ((), ())), preferred_element_type=F32)


def kernel(
    ny,
    nx,
    nt,
    prompt_ref,
    owner_ref,
    plen_ref,
    rlen_ref,
    q_hbm,
    k_hbm,
    v_hbm,
    o_hbm,
    do_hbm,
    dq,
    dk,
    dv,
    q,
    k,
    v,
    o,
    do,
    strip,
    cut,
    units,
    picked,
    pre,
    back_out,
    back,
    sums,
    parts,
    final,
    spread,
    partial,
    sources,
    exps,
    prods,
    ds_pre,
    w_low,
    ds_low,
    delta,
    total,
    known,
    in_sem,
    send_sem,
    recv_sem,
):
    n_seq = ny * nx
    group = nx * nt
    heads = q.shape[1] // (nx * HEAD_SIZE)
    unit_rows = PREFIX_ROWS // (nt // 2)
    width = heads * HEAD_SIZE
    factor = 1.0 / math.sqrt(HEAD_SIZE)
    s = lax.axis_index("seq")
    t = lax.axis_index("head")
    y, x = lax.div(s, nx), lax.rem(s, nx)
    block, kind = lax.div(t, 2), lax.rem(t, 2)

    def each(count, body, start=0):
        def step(i, carry):
            body(i)
            return carry

        lax.fori_loop(start, count, step, 0)

    loads = [
        pltpu.make_async_copy(a, b, in_sem.at[i])
        for i, (a, b) in enumerate(((q_hbm, q), (k_hbm, k), (v_hbm, v), (do_hbm, do), (o_hbm, o)))
    ]
    for load in loads:
        load.start()

    barrier = pltpu.get_barrier_semaphore()

    nz = nt // 2
    xs = [lax.rem(x + i, nx) for i in range(nx)]
    ys = [lax.rem(y + i, ny) for i in range(ny)]
    zs = [lax.rem(block + i, nz) for i in range(nz)]
    cs = [kind, 1 - kind]

    def far_first(n):
        return sorted(range(n), key=lambda i: (-min(i, n - i), i))

    plane = [(i, j) for i in range(ny) for j in range(nx) if i + j > 0]
    plane.sort(key=lambda at: -min(at[0], ny - at[0]) - min(at[1], nx - at[1]))
    column = [(j, c) for j in far_first(nz) for c in (1, 0)]

    def greet(semaphore, peer):
        pl.semaphore_signal(semaphore, inc=1, device_id=peer, device_id_type=MESH)

    line_y = [(ys[i] * nx + x, t) for i in far_first(ny) if i > 0]
    line_x = [(y * nx + xs[i], t) for i in far_first(nx) if i > 0]
    line_t = [(s, zs[j] * 2 + cs[c]) for j, c in column if j + c > 0]
    for peer in line_t + line_y + line_x:
        greet(barrier, peer)
    pl.semaphore_wait(barrier, len(line_t) + len(line_y) + len(line_x))
    for peer in line_y + line_t:
        greet(known, peer)

    def remote(src, dst, stage, peer):
        return pltpu.make_async_remote_copy(
            src_ref=src,
            dst_ref=dst,
            send_sem=send_sem.at[stage],
            recv_sem=recv_sem.at[stage],
            device_id=peer,
            device_id_type=MESH,
        )

    def local(src, dst, stage):
        return pltpu.make_async_copy(src, dst, recv_sem.at[stage])

    def arrived(ref, stage):
        pltpu.make_async_copy(ref, ref, recv_sem.at[stage]).wait()

    def sent(ref, stage):
        pltpu.make_async_copy(ref, ref, send_sem.at[stage]).wait()

    @pl.when(t == 0)
    def _():
        for i in far_first(nz):
            rows = pl.ds(i * unit_rows, unit_rows)
            if i > 0:
                remote(k_hbm.at[rows], strip, 0, (s, 2 * i)).start()
            else:
                local(k_hbm.at[rows], strip, 0).start()
            remote(v_hbm.at[rows], strip, 0, (s, 2 * i + 1)).start()

    for i in range(nx):
        s2 = y * nx + xs[i]
        sources[i * nt] = s2
        for t2 in range(1, nt):
            sources[i * nt + t2] = owner_ref[prompt_ref[s2 * (nt - 1) + (t2 - 1)]]

    lane = lax.broadcasted_iota(jnp.int32, (8, group * unit_rows), 1) // unit_rows
    source_line = jnp.zeros_like(lane)
    for i in range(group):
        source_line = jnp.where(lane == i, sources[i], source_line)
    shape = (unit_rows, group * unit_rows)
    same_row = (
        lax.broadcasted_iota(jnp.int32, shape, 0)
        == lax.broadcasted_iota(jnp.int32, shape, 1) % unit_rows
    )
    keyed = jnp.where(same_row, jnp.broadcast_to(source_line[:1], shape), -1)

    def spread_rows(i):
        spread[pl.ds(pl.multiple_of(i * unit_rows, unit_rows), unit_rows), :] = jnp.where(
            keyed == i, 1.0, 0.0
        ).astype(BF16)

    each(n_seq, spread_rows)

    is_prefix = t == 0
    mine = s * (nt - 1) + jnp.maximum(t - 1, 0)
    own_len = lax.fori_loop(
        0, n_seq, lambda i, n: n + jnp.where(owner_ref[i] == s, plen_ref[i], 0), jnp.int32(0)
    )
    live = jnp.where(is_prefix, own_len, rlen_ref[jnp.maximum(t - 1, 0), s])
    live_local = jnp.where(is_prefix, 0, live)
    prefix_count = jnp.where(is_prefix, PREFIX_ROWS, plen_ref[prompt_ref[mine]])
    slack = jnp.where(is_prefix, 0, PREFIX_ROWS)
    pair = 2 * HEAD_SIZE
    key_at = lax.broadcasted_iota(jnp.int32, (RLEN, pair), 0)
    row_at = lax.broadcasted_iota(jnp.int32, (RLEN, pair), 1) % RLEN
    row_line = lax.broadcasted_iota(jnp.int32, (1, pair), 1) % RLEN

    def columns(ref, g, p):
        at = pl.multiple_of(g * width + p * pair, HEAD_SIZE)
        return jnp.concatenate(
            [ref[:, pl.ds(at, HEAD_SIZE)], ref[:, pl.ds(at + HEAD_SIZE, HEAD_SIZE)]], axis=0
        )

    def head_columns(ref, g):
        return ref[:, pl.ds(pl.multiple_of(g * HEAD_SIZE, HEAD_SIZE), HEAD_SIZE)]

    def powers(key_rows, query_rows, allowed):
        scores = mm(key_rows, query_rows, 1, 1) * (factor * math.log2(math.e))
        return jnp.where(allowed, jnp.exp2(scores), 0.0)

    def own_part(g):
        allowed = (key_at <= row_at) & (row_at < live_local)
        key_rows, value_rows = head_columns(k, g), head_columns(v, g)
        ones = jnp.ones((8, HEAD_SIZE), BF16)
        for p in range(heads // 2):
            at = pl.ds(p * pair, pair)
            grad_rows = columns(do, g, p)
            product = grad_rows.astype(F32) * columns(o, g, p).astype(F32)
            high = product.astype(BF16)
            low = (product - high.astype(F32)).astype(BF16)
            deltas = (mm(ones, high, 1, 1) + mm(ones, low, 1, 1)).astype(BF16).astype(F32)
            delta[g, :, at] = deltas
            raised = powers(key_rows, columns(q, g, p), allowed)
            total[g, :, at] = jnp.broadcast_to(jnp.sum(raised, axis=0, keepdims=True), (8, pair))
            exps[g, :, at] = raised
            prods[g, :, at] = raised * (mm(value_rows, grad_rows, 1, 1) - deltas[:1])

    def stack(ref, g):
        at = pl.multiple_of(g * width, HEAD_SIZE)
        return jnp.concatenate(
            [ref[:, pl.ds(at + h * HEAD_SIZE, HEAD_SIZE)] for h in range(heads)], axis=0
        )

    pl.semaphore_wait(known, len(line_y) + len(line_t))
    arrived(strip, 0)

    for h in range(nx):
        cut[h] = strip[:, h * HEAD_SIZE : (h + 1) * HEAD_SIZE]
    local(cut.at[x], units.at[s], 1).start()
    for i, j in plane:
        remote(cut.at[xs[j]], units.at[s], 1, (ys[i] * nx + xs[j], t)).start()

    for load in loads:
        load.wait()
    own_part(0)
    each(nx // 2, own_part, 1)

    arrived(units, 1)

    landing = pre.at[kind, x, pl.ds(pl.multiple_of(block * unit_rows, unit_rows), unit_rows)]
    for i in far_first(nx):
        for t2 in range(nt):
            picked[i * nt + t2] = units[sources[i * nt + t2]]
        for j, c in column:
            t2 = zs[j] * 2 + cs[c]
            if i + j + c == 0:
                local(picked.at[t], landing, 7).start()
            else:
                remote(picked.at[i * nt + t2], landing, 7 + i, (y * nx + xs[i], t2)).start()
    each(nx, own_part, nx // 2)

    def prefix_part(i):
        g = xs[(nx - i) % nx]
        arrived(pre.at[:, g], 7 + i)
        allowed = (row_at < live) & (key_at < prefix_count) & (key_at <= row_at + slack)
        key_rows, value_rows = pre[0, g], pre[1, g]
        for p in range(heads // 2):
            at = pl.ds(p * pair, pair)
            raised = powers(key_rows, columns(q, g, p), allowed)
            row_total = total[g, :1, at] + jnp.sum(raised, axis=0, keepdims=True)
            inverse = 1.0 / jnp.where(row_line < live, row_total, 1.0)
            total[g, :, at] = jnp.broadcast_to(inverse, (8, pair))
            weights = raised * inverse
            w_low[:, at] = weights.astype(BF16)
            grad_weights = mm(value_rows, columns(do, g, p), 1, 1)
            ds_pre[g, :, at] = (weights * (grad_weights - delta[g, :1, at])).astype(BF16)
        back_out[1, g] = mm(w_low[...], stack(do, g), 1, 0).astype(BF16)
        back_out[0, g] = (mm(ds_pre[g], stack(q, g), 1, 0) * factor).astype(BF16)

        for j, c in column:
            t2 = zs[j] * 2 + cs[c]
            unit = back_out.at[
                cs[c], g, pl.ds(pl.multiple_of(zs[j] * unit_rows, unit_rows), unit_rows)
            ]
            if i + j + c == 0:
                local(unit, back.at[t], 7 + nx).start()
            else:
                remote(unit, back.at[i * nt + t], 7 + nx + i, (y * nx + g, t2)).start()

    for i in far_first(nx):
        prefix_part(i)

    def rest(g):
        key_rows, prefix_rows = head_columns(k, g), pre[0, g]
        for p in range(heads // 2):
            at = pl.ds(p * pair, pair)
            inverse = total[g, :1, at]
            w_low[:, at] = (exps[g, :, at] * inverse).astype(BF16)
            low = (prods[g, :, at] * inverse).astype(BF16)
            ds_low[:, at] = low
            grads = mm(ds_pre[g, :, at], prefix_rows, 0, 0) + mm(low, key_rows, 0, 0)
            grads = (grads * factor).astype(BF16)
            to = pl.multiple_of(g * width + p * pair, HEAD_SIZE)
            dq[:, pl.ds(to, HEAD_SIZE)] = grads[:RLEN]
            dq[:, pl.ds(to + HEAD_SIZE, HEAD_SIZE)] = grads[RLEN:]
        to = pl.ds(pl.multiple_of(g * HEAD_SIZE, HEAD_SIZE), HEAD_SIZE)

        @pl.when(t != 0)
        def _():
            dv[:, to] = mm(w_low[...], stack(do, g), 1, 0).astype(BF16)
            dk[:, to] = (mm(ds_low[...], stack(q, g), 1, 0) * factor).astype(BF16)

    each(nx, rest)

    depth = nt * unit_rows
    for n, i in enumerate(far_first(nx)):
        arrived(back.at[pl.ds(i * nt, nt)], 7 + nx + i)
        gathered = back[pl.ds(i * nt, nt)].reshape(depth, HEAD_SIZE)
        added = mm(spread[:, pl.ds(i * depth, depth)], gathered, 1, 0)
        if n > 0:
            added += partial[...]
        if n < nx - 1:
            partial[...] = added
        else:
            sums[...] = added.astype(BF16).reshape(sums.shape)
    local(sums.at[s], parts.at[s], 4).start()

    for i, j in plane:
        s2 = ys[i] * nx + xs[j]
        remote(sums.at[s2], parts.at[s], 4, (s2, t)).start()
    arrived(parts, 4)
    for h in range(nx):
        whole = parts[h].astype(F32)
        for i in range(1, ny):
            whole += parts[i * nx + h].astype(F32)
        final[:, pl.ds(h * HEAD_SIZE, HEAD_SIZE)] = whole.astype(BF16)

    rows = pl.ds(pl.multiple_of(block * unit_rows, unit_rows), unit_rows)

    @pl.when(t == 0)
    def _():
        local(final, dk.at[rows], 5).start()

    @pl.when((t != 0) & (kind == 0))
    def _():
        remote(final, dk.at[rows], 5, (s, 0)).start()

    @pl.when(kind == 1)
    def _():
        remote(final, dv.at[rows], 6, (s, 0)).start()

    sent(units.at[pl.ds(0, n_seq - 1)], 1)
    for i in range(nx):
        count = nt if i > 0 else nt - 1
        sent(picked.at[pl.ds(0, count)], 7 + i)
        sent(back.at[pl.ds(0, count)], 7 + nx + i)
    sent(sums.at[pl.ds(0, n_seq - 1)], 4)

    @pl.when(t == 0)
    def _():
        sent(picked.at[pl.ds(0, (nt - 1) * nx)], 0)
        arrived(dk, 5)
        arrived(dv, 6)

    @pl.when((t != 0) & (kind == 0))
    def _():
        sent(final, 5)

    @pl.when(kind == 1)
    def _():
        sent(final, 6)


def shards(
    queries,
    key_matrix,
    value_matrix,
    attn_output,
    grad_output,
    prefix_len,
    rollout_len,
    rollout_prompt,
    prefix_owner,
):
    nt = lax.axis_size("head")
    n_seq = lax.axis_size("seq")
    nx = KEY_VALUE_HEADS
    ny = n_seq // nx
    group = nx * nt
    heads = QUERY_HEADS // nx
    width = heads * HEAD_SIZE
    unit_rows = PREFIX_ROWS // (nt // 2)
    unit = (unit_rows, HEAD_SIZE)
    anywhere = pl.BlockSpec(memory_space=pl.ANY)
    scalars = pl.BlockSpec(memory_space=pltpu.SMEM)
    resident = pl.BlockSpec(memory_space=pltpu.VMEM)
    wide = pltpu.VMEM(queries.shape, BF16)
    narrow = pltpu.VMEM(key_matrix.shape, BF16)
    per_head = (nx, RLEN, width)
    return pl.pallas_call(
        functools.partial(kernel, ny, nx, nt),
        out_shape=[wide, narrow, narrow],
        in_specs=[scalars] * 4 + [anywhere] * 5,
        out_specs=[resident] * 3,
        scratch_shapes=[
            wide,
            narrow,
            narrow,
            wide,
            wide,
            pltpu.VMEM((unit_rows, nx * HEAD_SIZE), BF16),
            pltpu.VMEM((nx,) + unit, BF16),
            pltpu.VMEM((n_seq,) + unit, BF16),
            pltpu.VMEM((group,) + unit, BF16),
            pltpu.VMEM((2, nx, PREFIX_ROWS, HEAD_SIZE), BF16),
            pltpu.VMEM((2, nx, PREFIX_ROWS, HEAD_SIZE), BF16),
            pltpu.VMEM((group,) + unit, BF16),
            pltpu.VMEM((n_seq,) + unit, BF16),
            pltpu.VMEM((n_seq,) + unit, BF16),
            pltpu.VMEM((unit_rows, nx * HEAD_SIZE), BF16),
            pltpu.VMEM((n_seq * unit_rows, group * unit_rows), BF16),
            pltpu.VMEM((n_seq * unit_rows, HEAD_SIZE), F32),
            pltpu.SMEM((group,), jnp.int32),
            pltpu.VMEM(per_head, F32),
            pltpu.VMEM(per_head, F32),
            pltpu.VMEM(per_head, BF16),
            pltpu.VMEM(per_head[1:], BF16),
            pltpu.VMEM(per_head[1:], BF16),
            pltpu.VMEM((nx, 8, width), F32),
            pltpu.VMEM((nx, 8, width), F32),
            pltpu.SemaphoreType.REGULAR,
            pltpu.SemaphoreType.DMA((5,)),
            pltpu.SemaphoreType.DMA((7 + 2 * nx,)),
            pltpu.SemaphoreType.DMA((7 + 2 * nx,)),
        ],
        compiler_params=pltpu.CompilerParams(
            collective_id=0, has_side_effects=True, vmem_limit_bytes=VMEM_BYTES
        ),
        name="attention_backward",
    )(
        rollout_prompt.reshape(-1),
        prefix_owner,
        prefix_len,
        rollout_len.T,
        queries,
        key_matrix,
        value_matrix,
        attn_output,
        grad_output,
    )


def solution(mesh):
    rows = P(("seq", "head"), None)
    return jax.shard_map(
        shards,
        mesh=mesh,
        in_specs=(rows,) * 5 + (P(),) * 4,
        out_specs=(rows,) * 3,
        check_vma=False,
    )
```

```python
import functools
import math

import jax
import jax.numpy as jnp
from jax import lax
from jax.experimental import pallas as pl
from jax.experimental.pallas import tpu as pltpu
from jax.sharding import PartitionSpec as P

QUERY_HEADS = 32
KEY_VALUE_HEADS = 4
HEAD_SIZE = 128
PREFIX_ROWS = 128
RLEN = 128
MESH = pl.DeviceIdType.MESH
F32 = jnp.float32
BF16 = jnp.bfloat16
VMEM_BYTES = 56 * 1024 * 1024


def mm(a, b, da, db):
    return lax.dot_general(a, b, (((da,), (db,)), ((), ())), preferred_element_type=F32)


def kernel(
    ny,
    nx,
    nt,
    prompt_ref,
    owner_ref,
    plen_ref,
    rlen_ref,
    q_hbm,
    k_hbm,
    v_hbm,
    o_hbm,
    do_hbm,
    dq,
    dk,
    dv,
    q,
    k,
    v,
    o,
    do,
    strip,
    cut,
    units,
    picked,
    pre,
    back_out,
    back,
    sums,
    parts,
    final,
    spread,
    partial,
    sources,
    exps,
    prods,
    ds_pre,
    w_low,
    ds_low,
    delta,
    total,
    known,
    in_sem,
    send_sem,
    recv_sem,
):
    n_seq = ny * nx
    group = nx * nt
    heads = q.shape[1] // (nx * HEAD_SIZE)
    unit_rows = PREFIX_ROWS // (nt // 2)
    width = heads * HEAD_SIZE
    factor = 1.0 / math.sqrt(HEAD_SIZE)
    s = lax.axis_index("seq")
    t = lax.axis_index("head")
    y, x = lax.div(s, nx), lax.rem(s, nx)
    block, kind = lax.div(t, 2), lax.rem(t, 2)

    def each(count, body, start=0):
        def step(i, carry):
            body(i)
            return carry

        lax.fori_loop(start, count, step, 0)

    loads = [
        pltpu.make_async_copy(a, b, in_sem.at[i])
        for i, (a, b) in enumerate(((q_hbm, q), (k_hbm, k), (v_hbm, v), (do_hbm, do), (o_hbm, o)))
    ]
    for load in loads:
        load.start()

    barrier = pltpu.get_barrier_semaphore()

    nz = nt // 2
    xs = [lax.rem(x + i, nx) for i in range(nx)]
    ys = [lax.rem(y + i, ny) for i in range(ny)]
    zs = [lax.rem(block + i, nz) for i in range(nz)]
    cs = [kind, 1 - kind]

    def far_first(n):
        return sorted(range(n), key=lambda i: (-min(i, n - i), i))

    plane = [(i, j) for i in range(ny) for j in range(nx) if i + j > 0]
    plane.sort(key=lambda at: -min(at[0], ny - at[0]) - min(at[1], nx - at[1]))
    column = [(j, c) for j in far_first(nz) for c in (1, 0)]

    def greet(semaphore, peer):
        pl.semaphore_signal(semaphore, inc=1, device_id=peer, device_id_type=MESH)

    line_y = [(ys[i] * nx + x, t) for i in far_first(ny) if i > 0]
    line_x = [(y * nx + xs[i], t) for i in far_first(nx) if i > 0]
    line_t = [(s, zs[j] * 2 + cs[c]) for j, c in column if j + c > 0]
    for peer in line_t + line_y + line_x:
        greet(barrier, peer)
    pl.semaphore_wait(barrier, len(line_t) + len(line_y) + len(line_x))
    for peer in line_y + line_t:
        greet(known, peer)

    def remote(src, dst, stage, peer):
        return pltpu.make_async_remote_copy(
            src_ref=src,
            dst_ref=dst,
            send_sem=send_sem.at[stage],
            recv_sem=recv_sem.at[stage],
            device_id=peer,
            device_id_type=MESH,
        )

    def local(src, dst, stage):
        return pltpu.make_async_copy(src, dst, recv_sem.at[stage])

    def arrived(ref, stage):
        pltpu.make_async_copy(ref, ref, recv_sem.at[stage]).wait()

    def sent(ref, stage):
        pltpu.make_async_copy(ref, ref, send_sem.at[stage]).wait()

    @pl.when(t == 0)
    def _():
        loads[1].wait()
        loads[2].wait()
        for i in far_first(nz):
            rows = pl.ds(i * unit_rows, unit_rows)
            if i > 0:
                remote(k.at[rows], strip, 0, (s, 2 * i)).start()
            else:
                local(k.at[rows], strip, 0).start()
            remote(v.at[rows], strip, 0, (s, 2 * i + 1)).start()

    for i in range(nx):
        s2 = y * nx + xs[i]
        sources[i * nt] = s2
        for t2 in range(1, nt):
            sources[i * nt + t2] = owner_ref[prompt_ref[s2 * (nt - 1) + (t2 - 1)]]

    lane = lax.broadcasted_iota(jnp.int32, (8, group * unit_rows), 1) // unit_rows
    source_line = jnp.zeros_like(lane)
    for i in range(group):
        source_line = jnp.where(lane == i, sources[i], source_line)
    shape = (unit_rows, group * unit_rows)
    same_row = (
        lax.broadcasted_iota(jnp.int32, shape, 0)
        == lax.broadcasted_iota(jnp.int32, shape, 1) % unit_rows
    )
    keyed = jnp.where(same_row, jnp.broadcast_to(source_line[:1], shape), -1)

    def spread_rows(i):
        spread[pl.ds(pl.multiple_of(i * unit_rows, unit_rows), unit_rows), :] = jnp.where(
            keyed == i, 1.0, 0.0
        ).astype(BF16)

    each(n_seq, spread_rows)

    is_prefix = t == 0
    mine = s * (nt - 1) + jnp.maximum(t - 1, 0)
    own_len = lax.fori_loop(
        0, n_seq, lambda i, n: n + jnp.where(owner_ref[i] == s, plen_ref[i], 0), jnp.int32(0)
    )
    live = jnp.where(is_prefix, own_len, rlen_ref[jnp.maximum(t - 1, 0), s])
    live_local = jnp.where(is_prefix, 0, live)
    prefix_count = jnp.where(is_prefix, PREFIX_ROWS, plen_ref[prompt_ref[mine]])
    slack = jnp.where(is_prefix, 0, PREFIX_ROWS)
    pair = 2 * HEAD_SIZE
    key_at = lax.broadcasted_iota(jnp.int32, (RLEN, pair), 0)
    row_at = lax.broadcasted_iota(jnp.int32, (RLEN, pair), 1) % RLEN
    row_line = lax.broadcasted_iota(jnp.int32, (1, pair), 1) % RLEN

    def columns(ref, g, p):
        at = pl.multiple_of(g * width + p * pair, HEAD_SIZE)
        return jnp.concatenate(
            [ref[:, pl.ds(at, HEAD_SIZE)], ref[:, pl.ds(at + HEAD_SIZE, HEAD_SIZE)]], axis=0
        )

    def head_columns(ref, g):
        return ref[:, pl.ds(pl.multiple_of(g * HEAD_SIZE, HEAD_SIZE), HEAD_SIZE)]

    def powers(key_rows, query_rows, allowed):
        scores = mm(key_rows, query_rows, 1, 1) * (factor * math.log2(math.e))
        return jnp.where(allowed, jnp.exp2(scores), 0.0)

    def own_part(g):
        allowed = (key_at <= row_at) & (row_at < live_local)
        key_rows, value_rows = head_columns(k, g), head_columns(v, g)
        ones = jnp.ones((8, HEAD_SIZE), BF16)
        for p in range(heads // 2):
            at = pl.ds(p * pair, pair)
            grad_rows = columns(do, g, p)
            product = grad_rows.astype(F32) * columns(o, g, p).astype(F32)
            high = product.astype(BF16)
            low = (product - high.astype(F32)).astype(BF16)
            deltas = (mm(ones, high, 1, 1) + mm(ones, low, 1, 1)).astype(BF16).astype(F32)
            delta[g, :, at] = deltas
            raised = powers(key_rows, columns(q, g, p), allowed)
            total[g, :, at] = jnp.broadcast_to(jnp.sum(raised, axis=0, keepdims=True), (8, pair))
            exps[g, :, at] = raised
            prods[g, :, at] = raised * (mm(value_rows, grad_rows, 1, 1) - deltas[:1])

    def stack(ref, g):
        at = pl.multiple_of(g * width, HEAD_SIZE)
        return jnp.concatenate(
            [ref[:, pl.ds(at + h * HEAD_SIZE, HEAD_SIZE)] for h in range(heads)], axis=0
        )

    pl.semaphore_wait(known, len(line_y) + len(line_t))
    arrived(strip, 0)

    for h in range(nx):
        cut[h] = strip[:, h * HEAD_SIZE : (h + 1) * HEAD_SIZE]
    local(cut.at[x], units.at[s], 1).start()
    for i, j in plane:
        remote(cut.at[xs[j]], units.at[s], 1, (ys[i] * nx + xs[j], t)).start()

    @pl.when(t != 0)
    def _():
        loads[1].wait()
        loads[2].wait()

    for i in (0, 3, 4):
        loads[i].wait()
    own_part(0)
    each(nx // 2, own_part, 1)

    arrived(units, 1)

    landing = pre.at[kind, x, pl.ds(pl.multiple_of(block * unit_rows, unit_rows), unit_rows)]
    for i in far_first(nx):
        for t2 in range(nt):
            picked[i * nt + t2] = units[sources[i * nt + t2]]
        for j, c in column:
            t2 = zs[j] * 2 + cs[c]
            if i + j + c == 0:
                local(picked.at[t], landing, 7).start()
            else:
                remote(picked.at[i * nt + t2], landing, 7 + i, (y * nx + xs[i], t2)).start()
    each(nx, own_part, nx // 2)

    def prefix_part(i):
        g = xs[(nx - i) % nx]
        arrived(pre.at[:, g], 7 + i)
        allowed = (row_at < live) & (key_at < prefix_count) & (key_at <= row_at + slack)
        key_rows, value_rows = pre[0, g], pre[1, g]
        for p in range(heads // 2):
            at = pl.ds(p * pair, pair)
            raised = powers(key_rows, columns(q, g, p), allowed)
            row_total = total[g, :1, at] + jnp.sum(raised, axis=0, keepdims=True)
            inverse = 1.0 / jnp.where(row_line < live, row_total, 1.0)
            total[g, :, at] = jnp.broadcast_to(inverse, (8, pair))
            weights = raised * inverse
            w_low[:, at] = weights.astype(BF16)
            grad_weights = mm(value_rows, columns(do, g, p), 1, 1)
            ds_pre[g, :, at] = (weights * (grad_weights - delta[g, :1, at])).astype(BF16)
        back_out[1, g] = mm(w_low[...], stack(do, g), 1, 0).astype(BF16)
        back_out[0, g] = (mm(ds_pre[g], stack(q, g), 1, 0) * factor).astype(BF16)

        for j, c in column:
            t2 = zs[j] * 2 + cs[c]
            unit = back_out.at[
                cs[c], g, pl.ds(pl.multiple_of(zs[j] * unit_rows, unit_rows), unit_rows)
            ]
            if i + j + c == 0:
                local(unit, back.at[t], 7 + nx).start()
            else:
                remote(unit, back.at[i * nt + t], 7 + nx + i, (y * nx + g, t2)).start()

    for i in far_first(nx):
        prefix_part(i)

    def rest(g):
        key_rows, prefix_rows = head_columns(k, g), pre[0, g]
        for p in range(heads // 2):
            at = pl.ds(p * pair, pair)
            inverse = total[g, :1, at]
            w_low[:, at] = (exps[g, :, at] * inverse).astype(BF16)
            low = (prods[g, :, at] * inverse).astype(BF16)
            ds_low[:, at] = low
            grads = mm(ds_pre[g, :, at], prefix_rows, 0, 0) + mm(low, key_rows, 0, 0)
            grads = (grads * factor).astype(BF16)
            to = pl.multiple_of(g * width + p * pair, HEAD_SIZE)
            dq[:, pl.ds(to, HEAD_SIZE)] = grads[:RLEN]
            dq[:, pl.ds(to + HEAD_SIZE, HEAD_SIZE)] = grads[RLEN:]
        to = pl.ds(pl.multiple_of(g * HEAD_SIZE, HEAD_SIZE), HEAD_SIZE)

        @pl.when(t != 0)
        def _():
            dv[:, to] = mm(w_low[...], stack(do, g), 1, 0).astype(BF16)
            dk[:, to] = (mm(ds_low[...], stack(q, g), 1, 0) * factor).astype(BF16)

    each(nx, rest)

    depth = nt * unit_rows
    for n, i in enumerate(far_first(nx)):
        arrived(back.at[pl.ds(i * nt, nt)], 7 + nx + i)
        gathered = back[pl.ds(i * nt, nt)].reshape(depth, HEAD_SIZE)
        added = mm(spread[:, pl.ds(i * depth, depth)], gathered, 1, 0)
        if n > 0:
            added += partial[...]
        if n < nx - 1:
            partial[...] = added
        else:
            sums[...] = added.astype(BF16).reshape(sums.shape)
    local(sums.at[s], parts.at[s], 4).start()

    for i, j in plane:
        s2 = ys[i] * nx + xs[j]
        remote(sums.at[s2], parts.at[s], 4, (s2, t)).start()
    arrived(parts, 4)
    for h in range(nx):
        whole = parts[h].astype(F32)
        for i in range(1, ny):
            whole += parts[i * nx + h].astype(F32)
        final[:, pl.ds(h * HEAD_SIZE, HEAD_SIZE)] = whole.astype(BF16)

    rows = pl.ds(pl.multiple_of(block * unit_rows, unit_rows), unit_rows)

    @pl.when(t == 0)
    def _():
        local(final, dk.at[rows], 5).start()

    @pl.when((t != 0) & (kind == 0))
    def _():
        remote(final, dk.at[rows], 5, (s, 0)).start()

    @pl.when(kind == 1)
    def _():
        remote(final, dv.at[rows], 6, (s, 0)).start()

    sent(units.at[pl.ds(0, n_seq - 1)], 1)
    for i in range(nx):
        count = nt if i > 0 else nt - 1
        sent(picked.at[pl.ds(0, count)], 7 + i)
        sent(back.at[pl.ds(0, count)], 7 + nx + i)
    sent(sums.at[pl.ds(0, n_seq - 1)], 4)

    @pl.when(t == 0)
    def _():
        sent(picked.at[pl.ds(0, (nt - 1) * nx)], 0)
        arrived(dk, 5)
        arrived(dv, 6)

    @pl.when((t != 0) & (kind == 0))
    def _():
        sent(final, 5)

    @pl.when(kind == 1)
    def _():
        sent(final, 6)


def hand_over(dq, dk, dv, dq_out, dk_out, dv_out, sem):
    rows = dq.shape[0] // 4
    pairs = [(dq.at[pl.ds(i * rows, rows)], dq_out.at[pl.ds(i * rows, rows)]) for i in range(4)]
    copies = [
        pltpu.make_async_copy(a, b, sem.at[i])
        for i, (a, b) in enumerate(pairs + [(dk, dk_out), (dv, dv_out)])
    ]
    for copy in copies:
        copy.start()
    for copy in copies:
        copy.wait()


def shards(
    queries,
    key_matrix,
    value_matrix,
    attn_output,
    grad_output,
    prefix_len,
    rollout_len,
    rollout_prompt,
    prefix_owner,
):
    nt = lax.axis_size("head")
    n_seq = lax.axis_size("seq")
    nx = KEY_VALUE_HEADS
    ny = n_seq // nx
    group = nx * nt
    heads = QUERY_HEADS // nx
    width = heads * HEAD_SIZE
    unit_rows = PREFIX_ROWS // (nt // 2)
    unit = (unit_rows, HEAD_SIZE)
    anywhere = pl.BlockSpec(memory_space=pl.ANY)
    scalars = pl.BlockSpec(memory_space=pltpu.SMEM)
    resident = pl.BlockSpec(memory_space=pltpu.VMEM)
    wide = pltpu.VMEM(queries.shape, BF16)
    narrow = pltpu.VMEM(key_matrix.shape, BF16)
    per_head = (nx, RLEN, width)
    grads = pl.pallas_call(
        functools.partial(kernel, ny, nx, nt),
        out_shape=[wide, narrow, narrow],
        in_specs=[scalars] * 4 + [anywhere] * 5,
        out_specs=[resident] * 3,
        scratch_shapes=[
            wide,
            narrow,
            narrow,
            wide,
            wide,
            pltpu.VMEM((unit_rows, nx * HEAD_SIZE), BF16),
            pltpu.VMEM((nx,) + unit, BF16),
            pltpu.VMEM((n_seq,) + unit, BF16),
            pltpu.VMEM((group,) + unit, BF16),
            pltpu.VMEM((2, nx, PREFIX_ROWS, HEAD_SIZE), BF16),
            pltpu.VMEM((2, nx, PREFIX_ROWS, HEAD_SIZE), BF16),
            pltpu.VMEM((group,) + unit, BF16),
            pltpu.VMEM((n_seq,) + unit, BF16),
            pltpu.VMEM((n_seq,) + unit, BF16),
            pltpu.VMEM((unit_rows, nx * HEAD_SIZE), BF16),
            pltpu.VMEM((n_seq * unit_rows, group * unit_rows), BF16),
            pltpu.VMEM((n_seq * unit_rows, HEAD_SIZE), F32),
            pltpu.SMEM((group,), jnp.int32),
            pltpu.VMEM(per_head, F32),
            pltpu.VMEM(per_head, F32),
            pltpu.VMEM(per_head, BF16),
            pltpu.VMEM(per_head[1:], BF16),
            pltpu.VMEM(per_head[1:], BF16),
            pltpu.VMEM((nx, 8, width), F32),
            pltpu.VMEM((nx, 8, width), F32),
            pltpu.SemaphoreType.REGULAR,
            pltpu.SemaphoreType.DMA((5,)),
            pltpu.SemaphoreType.DMA((7 + 2 * nx,)),
            pltpu.SemaphoreType.DMA((7 + 2 * nx,)),
        ],
        compiler_params=pltpu.CompilerParams(
            collective_id=0, has_side_effects=True, vmem_limit_bytes=VMEM_BYTES
        ),
        name="attention_backward",
    )(
        rollout_prompt.reshape(-1),
        prefix_owner,
        prefix_len,
        rollout_len.T,
        queries,
        key_matrix,
        value_matrix,
        attn_output,
        grad_output,
    )
    grads = [pltpu.with_memory_space_constraint(grad, pltpu.VMEM) for grad in grads]
    return pl.pallas_call(
        hand_over,
        out_shape=[jax.ShapeDtypeStruct(grad.shape, BF16) for grad in grads],
        in_specs=[resident] * 3,
        out_specs=[anywhere] * 3,
        scratch_shapes=[pltpu.SemaphoreType.DMA((6,))],
        compiler_params=pltpu.CompilerParams(vmem_limit_bytes=VMEM_BYTES),
        name="hand_over",
    )(*grads)


def solution(mesh):
    rows = P(("seq", "head"), None)
    return jax.shard_map(
        shards,
        mesh=mesh,
        in_specs=(rows,) * 5 + (P(),) * 4,
        out_specs=(rows,) * 3,
        check_vma=False,
    )
```

```python
import functools
import math

import jax
import jax.numpy as jnp
from jax import lax
from jax.experimental import pallas as pl
from jax.experimental.pallas import tpu as pltpu
from jax.sharding import PartitionSpec as P

QUERY_HEADS = 32
KEY_VALUE_HEADS = 4
HEAD_SIZE = 128
PREFIX_ROWS = 128
RLEN = 128
MESH = pl.DeviceIdType.MESH
F32 = jnp.float32
BF16 = jnp.bfloat16
VMEM_BYTES = 56 * 1024 * 1024


def mm(a, b, da, db):
    return lax.dot_general(a, b, (((da,), (db,)), ((), ())), preferred_element_type=F32)


def kernel(
    ny,
    nx,
    nt,
    prompt_ref,
    owner_ref,
    plen_ref,
    rlen_ref,
    q_hbm,
    k_hbm,
    v_hbm,
    o_hbm,
    do_hbm,
    dq,
    dk,
    dv,
    q,
    k,
    v,
    o,
    do,
    strip,
    cut,
    units,
    picked,
    pre,
    back_out,
    back,
    sums,
    parts,
    final,
    spread,
    partial,
    sources,
    exps,
    prods,
    ds_pre,
    w_low,
    ds_low,
    delta,
    total,
    known,
    in_sem,
    send_sem,
    recv_sem,
):
    n_seq = ny * nx
    group = nx * nt
    heads = q.shape[1] // (nx * HEAD_SIZE)
    unit_rows = PREFIX_ROWS // (nt // 2)
    width = heads * HEAD_SIZE
    factor = 1.0 / math.sqrt(HEAD_SIZE)
    s = lax.axis_index("seq")
    t = lax.axis_index("head")
    y, x = lax.div(s, nx), lax.rem(s, nx)
    block, kind = lax.div(t, 2), lax.rem(t, 2)

    def each(count, body, start=0):
        def step(i, carry):
            body(i)
            return carry

        lax.fori_loop(start, count, step, 0)

    loads = [
        pltpu.make_async_copy(a, b, in_sem.at[i])
        for i, (a, b) in enumerate(((q_hbm, q), (k_hbm, k), (v_hbm, v), (do_hbm, do), (o_hbm, o)))
    ]
    barrier = pltpu.get_barrier_semaphore()

    nz = nt // 2
    xs = [lax.rem(x + i, nx) for i in range(nx)]
    ys = [lax.rem(y + i, ny) for i in range(ny)]
    zs = [lax.rem(block + i, nz) for i in range(nz)]
    cs = [kind, 1 - kind]

    def far_first(n):
        return sorted(range(n), key=lambda i: (-min(i, n - i), i))

    turns = [(n + 1) % nx for n in range(nx)]
    plane = [(i, j) for i in range(ny) for j in range(nx) if i + j > 0]
    plane.sort(key=lambda at: -min(at[0], ny - at[0]) - min(at[1], nx - at[1]))
    column = [(j, c) for j in far_first(nz) for c in (1, 0)]

    def greet(semaphore, peer):
        pl.semaphore_signal(semaphore, inc=1, device_id=peer, device_id_type=MESH)

    line_y = [(ys[i] * nx + x, t) for i in far_first(ny) if i > 0]
    line_x = [(y * nx + xs[i], t) for i in far_first(nx) if i > 0]
    line_t = [(s, zs[j] * 2 + cs[c]) for j, c in column if j + c > 0]
    pl.when(t != 0)(functools.partial(greet, barrier, (s, 0)))
    for peer in line_y + line_x:
        greet(barrier, peer)
    for peer in line_t:
        pl.when(peer[1] != 0)(functools.partial(greet, barrier, peer))
    for load in loads:
        load.start()
    pl.semaphore_wait(barrier, len(line_t) + len(line_y) + len(line_x))
    def remote(src, dst, stage, peer):
        return pltpu.make_async_remote_copy(
            src_ref=src,
            dst_ref=dst,
            send_sem=send_sem.at[stage],
            recv_sem=recv_sem.at[stage],
            device_id=peer,
            device_id_type=MESH,
        )

    def local(src, dst, stage):
        return pltpu.make_async_copy(src, dst, recv_sem.at[stage])

    def arrived(ref, stage):
        pltpu.make_async_copy(ref, ref, recv_sem.at[stage]).wait()

    def sent(ref, stage):
        pltpu.make_async_copy(ref, ref, send_sem.at[stage]).wait()

    @pl.when(t == 0)
    def _():
        loads[1].wait()
        loads[2].wait()
        for i in far_first(nz):
            rows = pl.ds(i * unit_rows, unit_rows)
            if i > 0:
                remote(k.at[rows], strip, 0, (s, 2 * i)).start()
            else:
                local(k.at[rows], strip, 0).start()
            remote(v.at[rows], strip, 0, (s, 2 * i + 1)).start()

    for peer in line_y + line_t:
        greet(known, peer)

    for i in range(nx):
        s2 = y * nx + xs[i]
        sources[i * nt] = s2
        for t2 in range(1, nt):
            sources[i * nt + t2] = owner_ref[prompt_ref[s2 * (nt - 1) + (t2 - 1)]]

    lane = lax.broadcasted_iota(jnp.int32, (8, group * unit_rows), 1) // unit_rows
    source_line = jnp.zeros_like(lane)
    for i in range(group):
        source_line = jnp.where(lane == i, sources[i], source_line)
    shape = (unit_rows, group * unit_rows)
    same_row = (
        lax.broadcasted_iota(jnp.int32, shape, 0)
        == lax.broadcasted_iota(jnp.int32, shape, 1) % unit_rows
    )
    keyed = jnp.where(same_row, jnp.broadcast_to(source_line[:1], shape), -1)

    def spread_rows(i):
        spread[pl.ds(pl.multiple_of(i * unit_rows, unit_rows), unit_rows), :] = jnp.where(
            keyed == i, 1.0, 0.0
        ).astype(BF16)

    each(n_seq, spread_rows)

    is_prefix = t == 0
    mine = s * (nt - 1) + jnp.maximum(t - 1, 0)
    own_len = lax.fori_loop(
        0, n_seq, lambda i, n: n + jnp.where(owner_ref[i] == s, plen_ref[i], 0), jnp.int32(0)
    )
    live = jnp.where(is_prefix, own_len, rlen_ref[jnp.maximum(t - 1, 0), s])
    live_local = jnp.where(is_prefix, 0, live)
    prefix_count = jnp.where(is_prefix, PREFIX_ROWS, plen_ref[prompt_ref[mine]])
    slack = jnp.where(is_prefix, 0, PREFIX_ROWS)
    pair = 2 * HEAD_SIZE
    key_at = lax.broadcasted_iota(jnp.int32, (RLEN, pair), 0)
    row_at = lax.broadcasted_iota(jnp.int32, (RLEN, pair), 1) % RLEN
    row_line = lax.broadcasted_iota(jnp.int32, (1, pair), 1) % RLEN

    def columns(ref, g, p):
        at = pl.multiple_of(g * width + p * pair, HEAD_SIZE)
        return jnp.concatenate(
            [ref[:, pl.ds(at, HEAD_SIZE)], ref[:, pl.ds(at + HEAD_SIZE, HEAD_SIZE)]], axis=0
        )

    def head_columns(ref, g):
        return ref[:, pl.ds(pl.multiple_of(g * HEAD_SIZE, HEAD_SIZE), HEAD_SIZE)]

    def powers(key_rows, query_rows, allowed):
        scores = mm(key_rows, query_rows, 1, 1) * (factor * math.log2(math.e))
        return jnp.where(allowed, jnp.exp2(scores), 0.0)

    def own_part(g):
        allowed = (key_at <= row_at) & (row_at < live_local)
        key_rows, value_rows = head_columns(k, g), head_columns(v, g)
        ones = jnp.ones((8, HEAD_SIZE), BF16)
        for p in range(heads // 2):
            at = pl.ds(p * pair, pair)
            grad_rows = columns(do, g, p)
            product = grad_rows.astype(F32) * columns(o, g, p).astype(F32)
            high = product.astype(BF16)
            low = (product - high.astype(F32)).astype(BF16)
            deltas = (mm(ones, high, 1, 1) + mm(ones, low, 1, 1)).astype(BF16).astype(F32)
            delta[g, :, at] = deltas
            raised = powers(key_rows, columns(q, g, p), allowed)
            total[g, :, at] = jnp.broadcast_to(jnp.sum(raised, axis=0, keepdims=True), (8, pair))
            exps[g, :, at] = raised
            prods[g, :, at] = raised * (mm(value_rows, grad_rows, 1, 1) - deltas[:1])

    def stack(ref, g):
        at = pl.multiple_of(g * width, HEAD_SIZE)
        return jnp.concatenate(
            [ref[:, pl.ds(at + h * HEAD_SIZE, HEAD_SIZE)] for h in range(heads)], axis=0
        )

    pl.semaphore_wait(known, len(line_y) + len(line_t))
    arrived(strip, 0)

    for h in range(nx):
        cut[h] = strip[:, h * HEAD_SIZE : (h + 1) * HEAD_SIZE]
    local(cut.at[x], units.at[s], 1).start()
    for i, j in plane:
        remote(cut.at[xs[j]], units.at[s], 1, (ys[i] * nx + xs[j], t)).start()

    @pl.when(t != 0)
    def _():
        loads[1].wait()
        loads[2].wait()

    for i in (0, 3, 4):
        loads[i].wait()
    own_part(0)
    each(nx // 2, own_part, 1)

    arrived(units, 1)

    landing = pre.at[kind, x, pl.ds(pl.multiple_of(block * unit_rows, unit_rows), unit_rows)]
    for i in turns:
        for t2 in range(nt):
            picked[i * nt + t2] = units[sources[i * nt + t2]]
        for j, c in column:
            t2 = zs[j] * 2 + cs[c]
            if i + j + c == 0:
                pl.when(t != 0)(local(picked.at[t], landing, 7).start)
            else:
                copy = remote(picked.at[i * nt + t2], landing, 7 + i, (y * nx + xs[i], t2))
                pl.when(t2 != 0)(copy.start)
    each(nx, own_part, nx // 2)

    @pl.when(t == 0)
    def _():
        for h in range(nx):
            pre[0, h] = k[:, h * HEAD_SIZE : (h + 1) * HEAD_SIZE]
            pre[1, h] = v[:, h * HEAD_SIZE : (h + 1) * HEAD_SIZE]


    def prefix_part(i):
        g = xs[(nx - i) % nx]
        pl.when(t != 0)(functools.partial(arrived, pre.at[:, g], 7 + i))
        allowed = (row_at < live) & (key_at < prefix_count) & (key_at <= row_at + slack)
        key_rows, value_rows = pre[0, g], pre[1, g]
        for p in range(heads // 2):
            at = pl.ds(p * pair, pair)
            raised = powers(key_rows, columns(q, g, p), allowed)
            row_total = total[g, :1, at] + jnp.sum(raised, axis=0, keepdims=True)
            inverse = 1.0 / jnp.where(row_line < live, row_total, 1.0)
            total[g, :, at] = jnp.broadcast_to(inverse, (8, pair))
            weights = raised * inverse
            w_low[:, at] = weights.astype(BF16)
            grad_weights = mm(value_rows, columns(do, g, p), 1, 1)
            ds_pre[g, :, at] = (weights * (grad_weights - delta[g, :1, at])).astype(BF16)
        back_out[1, g] = mm(w_low[...], stack(do, g), 1, 0).astype(BF16)
        back_out[0, g] = (mm(ds_pre[g], stack(q, g), 1, 0) * factor).astype(BF16)

        for j, c in column:
            t2 = zs[j] * 2 + cs[c]
            unit = back_out.at[
                cs[c], g, pl.ds(pl.multiple_of(zs[j] * unit_rows, unit_rows), unit_rows)
            ]
            if i + j + c == 0:
                local(unit, back.at[t], 7 + nx).start()
            else:
                remote(unit, back.at[i * nt + t], 7 + nx + i, (y * nx + g, t2)).start()

    for i in turns:
        prefix_part(i)

    def rest(g):
        key_rows, prefix_rows = head_columns(k, g), pre[0, g]
        for p in range(heads // 2):
            at = pl.ds(p * pair, pair)
            inverse = total[g, :1, at]
            w_low[:, at] = (exps[g, :, at] * inverse).astype(BF16)
            low = (prods[g, :, at] * inverse).astype(BF16)
            ds_low[:, at] = low
            grads = mm(ds_pre[g, :, at], prefix_rows, 0, 0) + mm(low, key_rows, 0, 0)
            grads = (grads * factor).astype(BF16)
            to = pl.multiple_of(g * width + p * pair, HEAD_SIZE)
            dq[:, pl.ds(to, HEAD_SIZE)] = grads[:RLEN]
            dq[:, pl.ds(to + HEAD_SIZE, HEAD_SIZE)] = grads[RLEN:]
        to = pl.ds(pl.multiple_of(g * HEAD_SIZE, HEAD_SIZE), HEAD_SIZE)

        @pl.when(t != 0)
        def _():
            dv[:, to] = mm(w_low[...], stack(do, g), 1, 0).astype(BF16)
            dk[:, to] = (mm(ds_low[...], stack(q, g), 1, 0) * factor).astype(BF16)

    each(nx, rest)

    depth = nt * unit_rows
    for n, i in enumerate(turns):
        arrived(back.at[pl.ds(i * nt, nt)], 7 + nx + i)
        gathered = back[pl.ds(i * nt, nt)].reshape(depth, HEAD_SIZE)
        added = mm(spread[:, pl.ds(i * depth, depth)], gathered, 1, 0)
        if n > 0:
            added += partial[...]
        if n < nx - 1:
            partial[...] = added
        else:
            sums[...] = added.astype(BF16).reshape(sums.shape)
    local(sums.at[s], parts.at[s], 4).start()

    for i, j in plane:
        s2 = ys[i] * nx + xs[j]
        remote(sums.at[s2], parts.at[s], 4, (s2, t)).start()
    arrived(parts, 4)
    for h in range(nx):
        whole = parts[h].astype(F32)
        for i in range(1, ny):
            whole += parts[i * nx + h].astype(F32)
        final[:, pl.ds(h * HEAD_SIZE, HEAD_SIZE)] = whole.astype(BF16)

    rows = pl.ds(pl.multiple_of(block * unit_rows, unit_rows), unit_rows)

    @pl.when(t == 0)
    def _():
        local(final, dk.at[rows], 5).start()

    @pl.when((t != 0) & (kind == 0))
    def _():
        remote(final, dk.at[rows], 5, (s, 0)).start()

    @pl.when(kind == 1)
    def _():
        remote(final, dv.at[rows], 6, (s, 0)).start()

    sent(units.at[pl.ds(0, n_seq - 1)], 1)
    for i in range(nx):
        count = nt if i > 0 else nt - 1
        if i > 0:
            sent(picked.at[pl.ds(0, nt - 1)], 7 + i)
        else:
            pl.when(t == 0)(functools.partial(sent, picked.at[pl.ds(0, nt - 1)], 7))
            pl.when(t != 0)(functools.partial(sent, picked.at[pl.ds(0, nt - 2)], 7))
        sent(back.at[pl.ds(0, count)], 7 + nx + i)
    sent(sums.at[pl.ds(0, n_seq - 1)], 4)

    @pl.when(t == 0)
    def _():
        sent(picked.at[pl.ds(0, (nt - 1) * nx)], 0)
        arrived(dk, 5)
        arrived(dv, 6)

    @pl.when((t != 0) & (kind == 0))
    def _():
        sent(final, 5)

    @pl.when(kind == 1)
    def _():
        sent(final, 6)


def hand_over(dq, dk, dv, dq_out, dk_out, dv_out, sem):
    rows = dq.shape[0] // 4
    pairs = [(dq.at[pl.ds(i * rows, rows)], dq_out.at[pl.ds(i * rows, rows)]) for i in range(4)]
    copies = [
        pltpu.make_async_copy(a, b, sem.at[i])
        for i, (a, b) in enumerate(pairs + [(dk, dk_out), (dv, dv_out)])
    ]
    for copy in copies:
        copy.start()
    for copy in copies:
        copy.wait()


def shards(
    queries,
    key_matrix,
    value_matrix,
    attn_output,
    grad_output,
    prefix_len,
    rollout_len,
    rollout_prompt,
    prefix_owner,
):
    nt = lax.axis_size("head")
    n_seq = lax.axis_size("seq")
    nx = KEY_VALUE_HEADS
    ny = n_seq // nx
    group = nx * nt
    heads = QUERY_HEADS // nx
    width = heads * HEAD_SIZE
    unit_rows = PREFIX_ROWS // (nt // 2)
    unit = (unit_rows, HEAD_SIZE)
    anywhere = pl.BlockSpec(memory_space=pl.ANY)
    scalars = pl.BlockSpec(memory_space=pltpu.SMEM)
    resident = pl.BlockSpec(memory_space=pltpu.VMEM)
    wide = pltpu.VMEM(queries.shape, BF16)
    narrow = pltpu.VMEM(key_matrix.shape, BF16)
    per_head = (nx, RLEN, width)
    grads = pl.pallas_call(
        functools.partial(kernel, ny, nx, nt),
        out_shape=[wide, narrow, narrow],
        in_specs=[scalars] * 4 + [anywhere] * 5,
        out_specs=[resident] * 3,
        scratch_shapes=[
            wide,
            narrow,
            narrow,
            wide,
            wide,
            pltpu.VMEM((unit_rows, nx * HEAD_SIZE), BF16),
            pltpu.VMEM((nx,) + unit, BF16),
            pltpu.VMEM((n_seq,) + unit, BF16),
            pltpu.VMEM((group,) + unit, BF16),
            pltpu.VMEM((2, nx, PREFIX_ROWS, HEAD_SIZE), BF16),
            pltpu.VMEM((2, nx, PREFIX_ROWS, HEAD_SIZE), BF16),
            pltpu.VMEM((group,) + unit, BF16),
            pltpu.VMEM((n_seq,) + unit, BF16),
            pltpu.VMEM((n_seq,) + unit, BF16),
            pltpu.VMEM((unit_rows, nx * HEAD_SIZE), BF16),
            pltpu.VMEM((n_seq * unit_rows, group * unit_rows), BF16),
            pltpu.VMEM((n_seq * unit_rows, HEAD_SIZE), F32),
            pltpu.SMEM((group,), jnp.int32),
            pltpu.VMEM(per_head, F32),
            pltpu.VMEM(per_head, F32),
            pltpu.VMEM(per_head, BF16),
            pltpu.VMEM(per_head[1:], BF16),
            pltpu.VMEM(per_head[1:], BF16),
            pltpu.VMEM((nx, 8, width), F32),
            pltpu.VMEM((nx, 8, width), F32),
            pltpu.SemaphoreType.REGULAR,
            pltpu.SemaphoreType.DMA((5,)),
            pltpu.SemaphoreType.DMA((7 + 2 * nx,)),
            pltpu.SemaphoreType.DMA((7 + 2 * nx,)),
        ],
        compiler_params=pltpu.CompilerParams(
            collective_id=0, has_side_effects=True, vmem_limit_bytes=VMEM_BYTES
        ),
        name="attention_backward",
    )(
        rollout_prompt.reshape(-1),
        prefix_owner,
        prefix_len,
        rollout_len.T,
        queries,
        key_matrix,
        value_matrix,
        attn_output,
        grad_output,
    )
    grads = [pltpu.with_memory_space_constraint(grad, pltpu.VMEM) for grad in grads]
    return pl.pallas_call(
        hand_over,
        out_shape=[jax.ShapeDtypeStruct(grad.shape, BF16) for grad in grads],
        in_specs=[resident] * 3,
        out_specs=[anywhere] * 3,
        scratch_shapes=[pltpu.SemaphoreType.DMA((6,))],
        compiler_params=pltpu.CompilerParams(vmem_limit_bytes=VMEM_BYTES),
        name="hand_over",
    )(*grads)


def solution(mesh):
    rows = P(("seq", "head"), None)
    return jax.shard_map(
        shards,
        mesh=mesh,
        in_specs=(rows,) * 5 + (P(),) * 4,
        out_specs=(rows,) * 3,
        check_vma=False,
    )
```

```python
import functools
import math

import jax
import jax.numpy as jnp
from jax import lax
from jax.experimental import pallas as pl
from jax.experimental.pallas import tpu as pltpu
from jax.sharding import PartitionSpec as P

QUERY_HEADS = 32
KEY_VALUE_HEADS = 4
HEAD_SIZE = 128
PREFIX_ROWS = 128
RLEN = 128
MESH = pl.DeviceIdType.MESH
F32 = jnp.float32
BF16 = jnp.bfloat16
VMEM_BYTES = 56 * 1024 * 1024


def mm(a, b, da, db):
    return lax.dot_general(a, b, (((da,), (db,)), ((), ())), preferred_element_type=F32)


def kernel(
    ny,
    nx,
    nt,
    prompt_ref,
    owner_ref,
    plen_ref,
    rlen_ref,
    q_hbm,
    k_hbm,
    v_hbm,
    o_hbm,
    do_hbm,
    dq,
    dk,
    dv,
    q,
    k,
    v,
    o,
    do,
    strip,
    cut,
    units,
    picked,
    pre,
    back_out,
    back,
    sums,
    parts,
    final,
    spread,
    partial,
    sources,
    exps,
    prods,
    ds_pre,
    w_low,
    ds_low,
    delta,
    total,
    known,
    in_sem,
    send_sem,
    recv_sem,
):
    n_seq = ny * nx
    group = nx * nt
    heads = q.shape[1] // (nx * HEAD_SIZE)
    unit_rows = PREFIX_ROWS // (nt // 2)
    width = heads * HEAD_SIZE
    factor = 1.0 / math.sqrt(HEAD_SIZE)
    s = lax.axis_index("seq")
    t = lax.axis_index("head")
    y, x = lax.div(s, nx), lax.rem(s, nx)
    block, kind = lax.div(t, 2), lax.rem(t, 2)

    def each(count, body, start=0):
        def step(i, carry):
            body(i)
            return carry

        lax.fori_loop(start, count, step, 0)

    loads = [
        pltpu.make_async_copy(a, b, in_sem.at[i])
        for i, (a, b) in enumerate(((q_hbm, q), (k_hbm, k), (v_hbm, v), (do_hbm, do), (o_hbm, o)))
    ]
    barrier = pltpu.get_barrier_semaphore()

    nz = nt // 2
    xs = [lax.rem(x + i, nx) for i in range(nx)]
    ys = [lax.rem(y + i, ny) for i in range(ny)]
    zs = [lax.rem(block + i, nz) for i in range(nz)]
    cs = [kind, 1 - kind]

    def far_first(n):
        return sorted(range(n), key=lambda i: (-min(i, n - i), i))

    turns = [(n + 1) % nx for n in range(nx)]
    plane = [(i, j) for i in range(ny) for j in range(nx) if i + j > 0]
    plane.sort(key=lambda at: -min(at[0], ny - at[0]) - min(at[1], nx - at[1]))
    column = [(j, c) for j in far_first(nz) for c in (1, 0)]

    def greet(semaphore, peer):
        pl.semaphore_signal(semaphore, inc=1, device_id=peer, device_id_type=MESH)

    line_y = [(ys[i] * nx + x, t) for i in far_first(ny) if i > 0]
    line_x = [(y * nx + xs[i], t) for i in far_first(nx) if i > 0]
    line_t = [(s, zs[j] * 2 + cs[c]) for j, c in column if j + c > 0]
    pl.when(t != 0)(functools.partial(greet, barrier, (s, 0)))
    for peer in line_y + line_x:
        greet(barrier, peer)
    for peer in line_t:
        pl.when(peer[1] != 0)(functools.partial(greet, barrier, peer))
    for load in loads:
        load.start()
    pl.semaphore_wait(barrier, len(line_t) + len(line_y) + len(line_x))
    def remote(src, dst, stage, peer):
        return pltpu.make_async_remote_copy(
            src_ref=src,
            dst_ref=dst,
            send_sem=send_sem.at[stage],
            recv_sem=recv_sem.at[stage],
            device_id=peer,
            device_id_type=MESH,
        )

    def local(src, dst, stage):
        return pltpu.make_async_copy(src, dst, recv_sem.at[stage])

    def arrived(ref, stage):
        pltpu.make_async_copy(ref, ref, recv_sem.at[stage]).wait()

    def sent(ref, stage):
        pltpu.make_async_copy(ref, ref, send_sem.at[stage]).wait()

    @pl.when(t == 0)
    def _():
        loads[1].wait()
        loads[2].wait()
        for i in far_first(nz):
            rows = pl.ds(i * unit_rows, unit_rows)
            if i > 0:
                remote(k.at[rows], strip, 0, (s, 2 * i)).start()
            else:
                local(k.at[rows], strip, 0).start()
            remote(v.at[rows], strip, 0, (s, 2 * i + 1)).start()

    for peer in line_y + line_t:
        greet(known, peer)

    for i in range(nx):
        s2 = y * nx + xs[i]
        sources[i * nt] = s2
        for t2 in range(1, nt):
            sources[i * nt + t2] = owner_ref[prompt_ref[s2 * (nt - 1) + (t2 - 1)]]

    lane = lax.broadcasted_iota(jnp.int32, (8, group * unit_rows), 1) // unit_rows
    source_line = jnp.zeros_like(lane)
    for i in range(group):
        source_line = jnp.where(lane == i, sources[i], source_line)
    shape = (unit_rows, group * unit_rows)
    same_row = (
        lax.broadcasted_iota(jnp.int32, shape, 0)
        == lax.broadcasted_iota(jnp.int32, shape, 1) % unit_rows
    )
    keyed = jnp.where(same_row, jnp.broadcast_to(source_line[:1], shape), -1)

    def spread_rows(i):
        spread[pl.ds(pl.multiple_of(i * unit_rows, unit_rows), unit_rows), :] = jnp.where(
            keyed == i, 1.0, 0.0
        ).astype(BF16)

    each(n_seq, spread_rows)

    is_prefix = t == 0
    mine = s * (nt - 1) + jnp.maximum(t - 1, 0)
    own_len = lax.fori_loop(
        0, n_seq, lambda i, n: n + jnp.where(owner_ref[i] == s, plen_ref[i], 0), jnp.int32(0)
    )
    live = jnp.where(is_prefix, own_len, rlen_ref[jnp.maximum(t - 1, 0), s])
    live_local = jnp.where(is_prefix, 0, live)
    prefix_count = jnp.where(is_prefix, PREFIX_ROWS, plen_ref[prompt_ref[mine]])
    slack = jnp.where(is_prefix, 0, PREFIX_ROWS)
    pair = 2 * HEAD_SIZE
    key_at = lax.broadcasted_iota(jnp.int32, (RLEN, pair), 0)
    row_at = lax.broadcasted_iota(jnp.int32, (RLEN, pair), 1) % RLEN
    row_line = lax.broadcasted_iota(jnp.int32, (1, pair), 1) % RLEN

    def columns(ref, g, p):
        at = pl.multiple_of(g * width + p * pair, HEAD_SIZE)
        return jnp.concatenate(
            [ref[:, pl.ds(at, HEAD_SIZE)], ref[:, pl.ds(at + HEAD_SIZE, HEAD_SIZE)]], axis=0
        )

    def head_columns(ref, g):
        return ref[:, pl.ds(pl.multiple_of(g * HEAD_SIZE, HEAD_SIZE), HEAD_SIZE)]

    def powers(key_rows, query_rows, allowed):
        scores = mm(key_rows, query_rows, 1, 1) * (factor * math.log2(math.e))
        return jnp.where(allowed, jnp.exp2(scores), 0.0)

    def own_part(g):
        allowed = (key_at <= row_at) & (row_at < live_local)
        key_rows, value_rows = head_columns(k, g), head_columns(v, g)
        ones = jnp.ones((8, HEAD_SIZE), BF16)
        for p in range(heads // 2):
            at = pl.ds(p * pair, pair)
            grad_rows = columns(do, g, p)
            product = grad_rows.astype(F32) * columns(o, g, p).astype(F32)
            high = product.astype(BF16)
            low = (product - high.astype(F32)).astype(BF16)
            deltas = (mm(ones, high, 1, 1) + mm(ones, low, 1, 1)).astype(BF16).astype(F32)
            delta[g, :, at] = deltas
            raised = powers(key_rows, columns(q, g, p), allowed)
            total[g, :, at] = jnp.broadcast_to(jnp.sum(raised, axis=0, keepdims=True), (8, pair))
            exps[g, :, at] = raised
            prods[g, :, at] = raised * (mm(value_rows, grad_rows, 1, 1) - deltas[:1])

    def stack(ref, g):
        at = pl.multiple_of(g * width, HEAD_SIZE)
        return jnp.concatenate(
            [ref[:, pl.ds(at + h * HEAD_SIZE, HEAD_SIZE)] for h in range(heads)], axis=0
        )

    pl.semaphore_wait(known, len(line_y) + len(line_t))
    arrived(strip, 0)

    for h in range(nx):
        cut[h] = strip[:, h * HEAD_SIZE : (h + 1) * HEAD_SIZE]
    local(cut.at[x], units.at[s], 1).start()
    for i, j in plane:
        remote(cut.at[xs[j]], units.at[s], 1, (ys[i] * nx + xs[j], t)).start()

    @pl.when(t != 0)
    def _():
        loads[1].wait()
        loads[2].wait()

    for i in (0, 3, 4):
        loads[i].wait()
    own_part(0)
    each(nx // 2, own_part, 1)

    arrived(units, 1)

    landing = pre.at[kind, x, pl.ds(pl.multiple_of(block * unit_rows, unit_rows), unit_rows)]
    for i in turns:
        for t2 in range(nt):
            picked[i * nt + t2] = units[sources[i * nt + t2]]
        for j, c in column:
            t2 = zs[j] * 2 + cs[c]
            if i + j + c == 0:
                pl.when(t != 0)(local(picked.at[t], landing, 7).start)
            else:
                copy = remote(picked.at[i * nt + t2], landing, 7 + i, (y * nx + xs[i], t2))
                pl.when(t2 != 0)(copy.start)
    each(nx, own_part, nx // 2)

    @pl.when(t == 0)
    def _():
        for h in range(nx):
            pre[0, h] = k[:, h * HEAD_SIZE : (h + 1) * HEAD_SIZE]
            pre[1, h] = v[:, h * HEAD_SIZE : (h + 1) * HEAD_SIZE]


    for i in range(nx):
        back[i * nt] = jnp.zeros((unit_rows, HEAD_SIZE), BF16)

    def prefix_part(i):
        g = xs[(nx - i) % nx]
        pl.when(t != 0)(functools.partial(arrived, pre.at[:, g], 7 + i))
        allowed = (row_at < live) & (key_at < prefix_count) & (key_at <= row_at + slack)
        key_rows, value_rows = pre[0, g], pre[1, g]
        for p in range(heads // 2):
            at = pl.ds(p * pair, pair)
            raised = powers(key_rows, columns(q, g, p), allowed)
            row_total = total[g, :1, at] + jnp.sum(raised, axis=0, keepdims=True)
            inverse = 1.0 / jnp.where(row_line < live, row_total, 1.0)
            total[g, :, at] = jnp.broadcast_to(inverse, (8, pair))
            weights = raised * inverse
            w_low[:, at] = weights.astype(BF16)
            grad_weights = mm(value_rows, columns(do, g, p), 1, 1)
            ds_pre[g, :, at] = (weights * (grad_weights - delta[g, :1, at])).astype(BF16)
        back_out[1, g] = mm(w_low[...], stack(do, g), 1, 0).astype(BF16)
        back_out[0, g] = (mm(ds_pre[g], stack(q, g), 1, 0) * factor).astype(BF16)

        for j, c in column:
            t2 = zs[j] * 2 + cs[c]
            unit = back_out.at[
                cs[c], g, pl.ds(pl.multiple_of(zs[j] * unit_rows, unit_rows), unit_rows)
            ]
            if i + j + c == 0:
                copy = local(unit, back.at[t], 7 + nx)
            else:
                copy = remote(unit, back.at[i * nt + t], 7 + nx + i, (y * nx + g, t2))
            pl.when(t != 0)(copy.start)

    for i in turns:
        prefix_part(i)

    def rest(g):
        key_rows, prefix_rows = head_columns(k, g), pre[0, g]
        for p in range(heads // 2):
            at = pl.ds(p * pair, pair)
            inverse = total[g, :1, at]
            w_low[:, at] = (exps[g, :, at] * inverse).astype(BF16)
            low = (prods[g, :, at] * inverse).astype(BF16)
            ds_low[:, at] = low
            grads = mm(ds_pre[g, :, at], prefix_rows, 0, 0) + mm(low, key_rows, 0, 0)
            grads = (grads * factor).astype(BF16)
            to = pl.multiple_of(g * width + p * pair, HEAD_SIZE)
            dq[:, pl.ds(to, HEAD_SIZE)] = grads[:RLEN]
            dq[:, pl.ds(to + HEAD_SIZE, HEAD_SIZE)] = grads[RLEN:]
        to = pl.ds(pl.multiple_of(g * HEAD_SIZE, HEAD_SIZE), HEAD_SIZE)

        @pl.when(t != 0)
        def _():
            dv[:, to] = mm(w_low[...], stack(do, g), 1, 0).astype(BF16)
            dk[:, to] = (mm(ds_low[...], stack(q, g), 1, 0) * factor).astype(BF16)

    each(nx, rest)

    depth = nt * unit_rows
    for n, i in enumerate(turns):
        arrived(back.at[pl.ds(i * nt + 1, nt - 1)], 7 + nx + i)
        gathered = back[pl.ds(i * nt, nt)].reshape(depth, HEAD_SIZE)
        added = mm(spread[:, pl.ds(i * depth, depth)], gathered, 1, 0)
        if n > 0:
            added += partial[...]
        if n < nx - 1:
            partial[...] = added
        else:
            sums[...] = added.astype(BF16).reshape(sums.shape)
    local(sums.at[s], parts.at[s], 4).start()

    for i, j in plane:
        s2 = ys[i] * nx + xs[j]
        remote(sums.at[s2], parts.at[s], 4, (s2, t)).start()
    arrived(parts, 4)
    for h in range(nx):
        whole = parts[h].astype(F32)
        for i in range(1, ny):
            whole += parts[i * nx + h].astype(F32)
        final[:, pl.ds(h * HEAD_SIZE, HEAD_SIZE)] = whole.astype(BF16)

    rows = pl.ds(pl.multiple_of(block * unit_rows, unit_rows), unit_rows)

    @pl.when(t == 0)
    def _():
        local(final, dk.at[rows], 5).start()

    @pl.when((t != 0) & (kind == 0))
    def _():
        remote(final, dk.at[rows], 5, (s, 0)).start()

    @pl.when(kind == 1)
    def _():
        remote(final, dv.at[rows], 6, (s, 0)).start()

    sent(units.at[pl.ds(0, n_seq - 1)], 1)
    for i in range(nx):
        count = nt if i > 0 else nt - 1
        if i > 0:
            sent(picked.at[pl.ds(0, nt - 1)], 7 + i)
        else:
            pl.when(t == 0)(functools.partial(sent, picked.at[pl.ds(0, nt - 1)], 7))
            pl.when(t != 0)(functools.partial(sent, picked.at[pl.ds(0, nt - 2)], 7))
        pl.when(t != 0)(functools.partial(sent, back.at[pl.ds(0, count)], 7 + nx + i))
    sent(sums.at[pl.ds(0, n_seq - 1)], 4)

    @pl.when(t == 0)
    def _():
        sent(picked.at[pl.ds(0, (nt - 1) * nx)], 0)
        arrived(dk, 5)
        arrived(dv, 6)
        for h in range(nx):
            at = pl.ds(h * HEAD_SIZE, HEAD_SIZE)
            dk[:, at] = (dk[:, at].astype(F32) + back_out[0, h].astype(F32)).astype(BF16)
            dv[:, at] = (dv[:, at].astype(F32) + back_out[1, h].astype(F32)).astype(BF16)

    @pl.when((t != 0) & (kind == 0))
    def _():
        sent(final, 5)

    @pl.when(kind == 1)
    def _():
        sent(final, 6)


def hand_over(dq, dk, dv, dq_out, dk_out, dv_out, sem):
    rows = dq.shape[0] // 4
    pairs = [(dq.at[pl.ds(i * rows, rows)], dq_out.at[pl.ds(i * rows, rows)]) for i in range(4)]
    copies = [
        pltpu.make_async_copy(a, b, sem.at[i])
        for i, (a, b) in enumerate(pairs + [(dk, dk_out), (dv, dv_out)])
    ]
    for copy in copies:
        copy.start()
    for copy in copies:
        copy.wait()


def shards(
    queries,
    key_matrix,
    value_matrix,
    attn_output,
    grad_output,
    prefix_len,
    rollout_len,
    rollout_prompt,
    prefix_owner,
):
    nt = lax.axis_size("head")
    n_seq = lax.axis_size("seq")
    nx = KEY_VALUE_HEADS
    ny = n_seq // nx
    group = nx * nt
    heads = QUERY_HEADS // nx
    width = heads * HEAD_SIZE
    unit_rows = PREFIX_ROWS // (nt // 2)
    unit = (unit_rows, HEAD_SIZE)
    anywhere = pl.BlockSpec(memory_space=pl.ANY)
    scalars = pl.BlockSpec(memory_space=pltpu.SMEM)
    resident = pl.BlockSpec(memory_space=pltpu.VMEM)
    wide = pltpu.VMEM(queries.shape, BF16)
    narrow = pltpu.VMEM(key_matrix.shape, BF16)
    per_head = (nx, RLEN, width)
    grads = pl.pallas_call(
        functools.partial(kernel, ny, nx, nt),
        out_shape=[wide, narrow, narrow],
        in_specs=[scalars] * 4 + [anywhere] * 5,
        out_specs=[resident] * 3,
        scratch_shapes=[
            wide,
            narrow,
            narrow,
            wide,
            wide,
            pltpu.VMEM((unit_rows, nx * HEAD_SIZE), BF16),
            pltpu.VMEM((nx,) + unit, BF16),
            pltpu.VMEM((n_seq,) + unit, BF16),
            pltpu.VMEM((group,) + unit, BF16),
            pltpu.VMEM((2, nx, PREFIX_ROWS, HEAD_SIZE), BF16),
            pltpu.VMEM((2, nx, PREFIX_ROWS, HEAD_SIZE), BF16),
            pltpu.VMEM((group,) + unit, BF16),
            pltpu.VMEM((n_seq,) + unit, BF16),
            pltpu.VMEM((n_seq,) + unit, BF16),
            pltpu.VMEM((unit_rows, nx * HEAD_SIZE), BF16),
            pltpu.VMEM((n_seq * unit_rows, group * unit_rows), BF16),
            pltpu.VMEM((n_seq * unit_rows, HEAD_SIZE), F32),
            pltpu.SMEM((group,), jnp.int32),
            pltpu.VMEM(per_head, F32),
            pltpu.VMEM(per_head, F32),
            pltpu.VMEM(per_head, BF16),
            pltpu.VMEM(per_head[1:], BF16),
            pltpu.VMEM(per_head[1:], BF16),
            pltpu.VMEM((nx, 8, width), F32),
            pltpu.VMEM((nx, 8, width), F32),
            pltpu.SemaphoreType.REGULAR,
            pltpu.SemaphoreType.DMA((5,)),
            pltpu.SemaphoreType.DMA((7 + 2 * nx,)),
            pltpu.SemaphoreType.DMA((7 + 2 * nx,)),
        ],
        compiler_params=pltpu.CompilerParams(
            collective_id=0, has_side_effects=True, vmem_limit_bytes=VMEM_BYTES
        ),
        name="attention_backward",
    )(
        rollout_prompt.reshape(-1),
        prefix_owner,
        prefix_len,
        rollout_len.T,
        queries,
        key_matrix,
        value_matrix,
        attn_output,
        grad_output,
    )
    grads = [pltpu.with_memory_space_constraint(grad, pltpu.VMEM) for grad in grads]
    return pl.pallas_call(
        hand_over,
        out_shape=[jax.ShapeDtypeStruct(grad.shape, BF16) for grad in grads],
        in_specs=[resident] * 3,
        out_specs=[anywhere] * 3,
        scratch_shapes=[pltpu.SemaphoreType.DMA((6,))],
        compiler_params=pltpu.CompilerParams(vmem_limit_bytes=VMEM_BYTES),
        name="hand_over",
    )(*grads)


def solution(mesh):
    rows = P(("seq", "head"), None)
    return jax.shard_map(
        shards,
        mesh=mesh,
        in_specs=(rows,) * 5 + (P(),) * 4,
        out_specs=(rows,) * 3,
        check_vma=False,
    )
```
